512 devices in a mesh: row: 32 (over z_hi, y, core), col: 16 (over z_lo, x).
Axes of the slice: x: 4, y: 4, z: 16 (z_hi: 4, z_lo: 4; z = z_hi * 4 + z_lo), core: 2. Of those that a mesh axis runs over, the one named last changes fastest.
Arguments:
- objects: float32 [2, 2, 4096, 4096], P(None, None, 'row', 'col'), may hold values from -4 to 4
- illumination: float32 [2, 128, 128], replicated, may hold values from -4 to 4
- intensity: float32 [2048, 128, 128], P(('row', 'col')), may hold values from 0 to 2
- row_offset: int32 [2048], P(('row', 'col')), may hold values from 0 to 127
- col_offset: int32 [2048], P(('row', 'col')), may hold values from 0 to 255
Outputs:
- object_grad: float32 [2, 2, 4096, 4096], P(None, None, 'row', 'col')
- probe_grad: float32 [2, 128, 128], replicated
The draws below stay inside these ranges and needn't reach their ends.
Inputs may be any that keep to these rules, and one draw needn't show every extreme that they name: `row_offset`: the row, within the tile of the device that holds position j, of the window's centre. `col_offset`: the column, within the tile of the device that holds position j, of the window's centre.
All inputs are finite; a program needn't handle non-finite values.
Results may differ from the reference program's by a relative error of at most 0.00013.
Values sent between devices are 32-bit elements; how exact they have to be, the bound alone decides.
A program may use at most 64 MiB of HBM per device.

```python
import math
import jax
import jax.numpy as jnp
from jax import lax

PROBE = 128
TH = 128
TW = 256
POS_DEV = 4
NY = 4096
NX = 4096
NPOS = 2048
N_ROW = 32
N_COL = 16


def with_ends(drawn, stream_key, smallest, high):
    extent = drawn.shape
    spot = [jax.random.randint(jax.random.fold_in(stream_key, axis), (), 0, extent[axis]) for axis in range(len(extent))]
    drawn = drawn.at[tuple(spot)].set(smallest)
    longest = extent.index(max(extent))
    spot[longest] = (spot[longest] + 1) % extent[longest]
    return drawn.at[tuple(spot)].set(high)


def block_scale(key, shape, shards, smallest, largest):
    gain = 1.0
    for dim, parts in shards:
        steps = jax.random.uniform(jax.random.fold_in(jax.random.fold_in(key, 6), dim), (parts,), jnp.float32, smallest / len(shards), largest / len(shards))
        gain = gain * jnp.repeat(jnp.exp(steps), shape[dim] // parts).reshape((-1,) + (1,) * (len(shape) - 1 - dim))
    return gain


def scatter_about(own_key, extent, width, limit, pieces=(), kind=jnp.bfloat16):
    drawn = width * jax.random.normal(own_key, extent, jnp.float32)
    if pieces:
        drawn = drawn * block_scale(own_key, extent, pieces, -0.22, 0.18)
    return jnp.clip(drawn, -limit, limit).astype(kind)


def setup_inputs(seed: int = 0) -> dict:
    key_of = jax.random.split(jax.random.key(seed), 6)
    objects = scatter_about(key_of[0], (2, 2, NY, NX), 0.7, 4.0, ((2, 32), (3, 16)), jnp.float32)
    illumination = scatter_about(key_of[1], (2, PROBE, PROBE), 0.7, 4.0, (), jnp.float32)
    intensity = jnp.clip(2.0 * jax.random.uniform(key_of[2], (NPOS, PROBE, PROBE), jnp.float32) ** block_scale(key_of[2], (NPOS, PROBE, PROBE), ((0, 512),), -0.2, 0.2), 0.0, 2.0)
    row_offset = with_ends(jax.random.randint(key_of[3], (NPOS,), 0, TH), jax.random.fold_in(key_of[3], 1), 0, TH - 1).astype(jnp.int32)
    col_offset = with_ends(jax.random.randint(key_of[4], (NPOS,), 0, TW), jax.random.fold_in(key_of[4], 1), 0, TW - 1).astype(jnp.int32)
    return dict(objects=objects, illumination=illumination, intensity=intensity, row_offset=row_offset, col_offset=col_offset)


depth = 0.5

def fresnel_phase(length):
    index = jnp.arange(length, dtype=jnp.int32)
    signed = jnp.where(index < length // 2, index, index - length)
    square = signed[:, None] ** 2 + signed[None, :] ** 2
    angle = -math.pi * depth / length * square.astype(jnp.float32)
    return (jnp.cos(angle), jnp.sin(angle))

def reference(objects, illumination, intensity, row_offset, col_offset):
    half_size = PROBE // 2
    cos_part, sin_part = fresnel_phase(PROBE)
    fresnel = lax.complex(cos_part, sin_part)
    object_field = lax.complex(objects[:, 0], objects[:, 1])
    padded = jnp.pad(object_field, ((0, 0), (half_size, half_size), (half_size, half_size)))
    probe_field = lax.complex(illumination[0], illumination[1])
    owner = jnp.arange(NPOS, dtype=jnp.int32) // POS_DEV
    row_start = (owner // N_COL * TH + row_offset).astype(jnp.int32)
    col_start = (owner % N_COL * TW + col_offset).astype(jnp.int32)
    anchor = jnp.zeros((), jnp.int32)

    def block_step(carry, first_index):
        total, probe_total = carry
        block_rows = lax.dynamic_slice_in_dim(row_start, first_index, POS_DEV)
        block_cols = lax.dynamic_slice_in_dim(col_start, first_index, POS_DEV)
        measured = lax.dynamic_slice_in_dim(intensity, first_index, POS_DEV, 0)

        def one_window(start_row, start_col):
            return lax.dynamic_slice(padded, (anchor, start_row, start_col), (2, PROBE, PROBE))
        windows = jax.vmap(one_window)(block_rows, block_cols)
        first_window = windows[:, 0]
        second_window = windows[:, 1]
        entry = probe_field * first_window
        moved = jnp.fft.ifft2(jnp.fft.fft2(entry, norm='ortho') * fresnel, norm='ortho')
        exit_wave = moved * second_window
        far_field = jnp.fft.fft2(exit_wave, norm='ortho')
        residual = jnp.real(far_field) ** 2 + jnp.imag(far_field) ** 2 - measured
        far_grad = residual * far_field
        exit_grad = jnp.fft.ifft2(far_grad, norm='ortho')
        moved_grad = jnp.conj(second_window) * exit_grad
        second_grad = jnp.conj(moved) * exit_grad
        entry_grad = jnp.fft.ifft2(jnp.fft.fft2(moved_grad, norm='ortho') * jnp.conj(fresnel), norm='ortho')
        first_grad = jnp.conj(probe_field) * entry_grad
        probe_total = probe_total + lax.optimization_barrier(jnp.sum(jnp.conj(first_window) * entry_grad, axis=0))
        stacked = jnp.stack([first_grad, second_grad], axis=1)

        def place(number, running):
            corner = (anchor, block_rows[number], block_cols[number])
            previous = lax.dynamic_slice(running, corner, (2, PROBE, PROBE))
            return lax.dynamic_update_slice(running, previous + stacked[number], corner)
        total = lax.fori_loop(0, POS_DEV, place, total)
        return ((total, probe_total), None)
    starts = jnp.arange(N_ROW * N_COL, dtype=jnp.int32) * POS_DEV
    initial = (jnp.zeros(padded.shape, padded.dtype), jnp.zeros((PROBE, PROBE), probe_field.dtype))
    (total, probe_total), unused = lax.scan(block_step, initial, starts)
    inner = total[:, half_size:half_size + NY, half_size:half_size + NX]
    object_grad = jnp.stack([jnp.real(inner), jnp.imag(inner)], axis=1)
    scaled = probe_total / math.sqrt(NPOS)
    probe_grad = jnp.stack([jnp.real(scaled), jnp.imag(scaled)])
    return (object_grad, probe_grad)
```

```python
import functools
import math

import jax
import jax.numpy as jnp
import ml_dtypes
import numpy as np
from jax import lax
from jax.experimental import pallas as pl
from jax.experimental.pallas import tpu as pltpu
from jax.sharding import PartitionSpec as P

depth = 0.5
side = 128
half = 64
tile_w = 256
count = 4
plane_rows = 8
plane_cols = 4
directions = ((-1, 0), (1, 0), (0, -1), (0, 1), (-1, -1), (-1, 1), (1, -1), (1, 1))
MESH = pl.DeviceIdType.MESH
f32 = jnp.float32
bf16 = jnp.bfloat16


def in_two(values):
    high = values.astype(ml_dtypes.bfloat16)
    low = (values - high.astype(np.float64)).astype(ml_dtypes.bfloat16)
    return high, low


def tables():
    index = np.arange(side)
    angle = -2.0 * math.pi / side * (index[:, None] * index[None, :] % side)
    real, imag = np.cos(angle) / math.sqrt(side), np.sin(angle) / math.sqrt(side)
    rows = np.block([[real, imag], [-imag, real]])
    cols = np.block([[real, -imag], [imag, real]])
    signed = np.where(index < side // 2, index, index - side)
    square = signed[:, None] ** 2 + signed[None, :] ** 2
    phase = -math.pi * depth / side * square
    fresnel = np.stack([np.cos(phase), np.sin(phase)]).astype(np.float32)
    return np.stack(in_two(rows) + in_two(cols)), fresnel


def split(values):
    high = values.astype(bf16)
    return high, (values - high.astype(f32)).astype(bf16)


def dot(left, right):
    return lax.dot_general(left, right, (((1,), (0,)), ((), ())), preferred_element_type=f32)


def kernel(
    mesh_shape,
    row_ref,
    col_ref,
    obj_ref,
    ill_ref,
    int_ref,
    tab_ref,
    fres_ref,
    og_ref,
    pg_ref,
    pad0,
    pad1,
    east_src,
    west_src,
    east_in,
    west_in,
    ill,
    inten,
    tab,
    fres,
    first_w,
    second_w,
    moved_s,
    acc0,
    acc1,
    fe_src,
    fw_src,
    ns_in,
    fe_in,
    fw_in,
    og,
    ar_src,
    ar_in,
    z_in,
    ar_out,
    local_sem,
    halo_send,
    halo_recv,
    fold_send,
    fold_recv,
    ar_send,
    ar_recv,
):
    n_row, n_col = mesh_shape
    row, col = lax.axis_index("row"), lax.axis_index("col")
    pads, accs = (pad0, pad1), (acc0, acc1)

    own = [
        [
            pltpu.make_async_copy(
                obj_ref.at[s, :, :, t * side : (t + 1) * side],
                pads[s].at[t + 1, :, half : half + side],
                local_sem.at[2 * s + t],
            )
            for t in range(2)
        ]
        for s in range(2)
    ]
    loads = [
        pltpu.make_async_copy(ill_ref, ill, local_sem.at[4]),
        pltpu.make_async_copy(tab_ref, tab, local_sem.at[5]),
        pltpu.make_async_copy(fres_ref, fres, local_sem.at[6]),
        pltpu.make_async_copy(int_ref, inten, local_sem.at[7]),
    ]
    for copy in own[0] + own[1] + loads:
        copy.start()

    def has(dr, dc):
        found = None
        if dr:
            found = (row > 0) if dr < 0 else (row < n_row - 1)
        if dc:
            col_found = (col > 0) if dc < 0 else (col < n_col - 1)
            found = col_found if found is None else jnp.logical_and(found, col_found)
        return found

    def halo_dst(s, dr, dc):
        if dc == 0:
            start = 3 * half if dr < 0 else 0
            return pads[s].at[1:3, :, start : start + half]
        into = west_in if dc > 0 else east_in
        start, size = ((half, side) if dr == 0 else (3 * half, half) if dr < 0 else (0, half))
        return into.at[s, start : start + size]

    def halo_copy(s, d):
        dr, dc = directions[d]
        if dc == 0:
            start = half if dr < 0 else side
            src = pads[s].at[1:3, :, start : start + half]
        else:
            start, size = ((0, side) if dr == 0 else (0, half) if dr < 0 else (half, half))
            src = (east_src if dc > 0 else west_src).at[s, start : start + size]
        return pltpu.make_async_remote_copy(
            src_ref=src,
            dst_ref=halo_dst(s, dr, dc),
            send_sem=halo_send.at[s, d],
            recv_sem=halo_recv.at[s, d],
            device_id=(row + dr, col + dc),
            device_id_type=MESH,
        )

    def fold_dst(s, dr, dc):
        if dc == 0:
            return ns_in.at[s, 1 if dr < 0 else 0]
        into = fw_in if dc > 0 else fe_in
        start, size = ((0, side) if dr == 0 else (3 * half, half) if dr < 0 else (side, half))
        return into.at[s, start : start + size]

    def fold_copy(s, d):
        dr, dc = directions[d]
        start, size = ((half, side) if dr == 0 else (0, half) if dr < 0 else (3 * half, half))
        if dc == 0:
            src = accs[s].at[:, start : start + size, 0:tile_w]
        else:
            src = (fe_src if dc > 0 else fw_src).at[s, start : start + size]
        return pltpu.make_async_remote_copy(
            src_ref=src,
            dst_ref=fold_dst(s, dr, dc),
            send_sem=fold_send.at[s, d],
            recv_sem=fold_recv.at[s, d],
            device_id=(row + dr, col + dc),
            device_id_type=MESH,
        )

    for dr, dc in directions:

        @pl.when(jnp.logical_not(has(-dr, -dc)))
        def _(dr=dr, dc=dc):
            for s in range(2):
                for dst in (halo_dst(s, dr, dc), fold_dst(s, dr, dc)):
                    dst[...] = jnp.zeros(dst.shape, f32)

    inner, outer = plane_rows * plane_cols, (n_row // plane_rows) * (n_col // plane_cols)
    outer_cols = n_col // plane_cols
    row_in, row_out = lax.rem(row, plane_rows), lax.div(row, plane_rows)
    col_in, col_out = lax.rem(col, plane_cols), lax.div(col, plane_cols)
    my_inner = row_in * plane_cols + col_in
    my_outer = row_out * outer_cols + col_out

    def inner_device(k):
        number = lax.rem(my_inner + k, inner)
        return number, (
            row_out * plane_rows + lax.div(number, plane_cols),
            col_out * plane_cols + lax.rem(number, plane_cols),
        )

    def outer_device(k):
        number = lax.rem(my_outer + k, outer)
        return number, (
            lax.div(number, outer_cols) * plane_rows + row_in,
            lax.rem(number, outer_cols) * plane_cols + col_in,
        )

    barrier = pltpu.get_barrier_semaphore()
    expected = jnp.int32(inner + outer - 2)
    for dr, dc in directions:
        found = has(dr, dc)
        expected = expected + found.astype(jnp.int32)

        @pl.when(found)
        def _(dr=dr, dc=dc):
            pl.semaphore_signal(
                barrier, inc=1, device_id=(row + dr, col + dc), device_id_type=MESH
            )

    def greet(device_of):
        def step(k, carry):
            pl.semaphore_signal(barrier, inc=1, device_id=device_of(k)[1], device_id_type=MESH)
            return carry

        return step

    lax.fori_loop(1, inner, greet(inner_device), 0)
    lax.fori_loop(1, outer, greet(outer_device), 0)

    def send_all(copy_of):
        for d in range(8):

            @pl.when(has(*directions[d]))
            def _(d=d):
                copy_of(d).start()

    def receive_all(copy_of):
        for d in range(8):
            dr, dc = directions[d]

            @pl.when(has(-dr, -dc))
            def _(d=d):
                copy_of(d).wait_recv()

    def sent_all(copy_of):
        for d in range(8):

            @pl.when(has(*directions[d]))
            def _(d=d):
                copy_of(d).wait_send()

    lane = lax.broadcasted_iota(jnp.int32, (1, side), 1)
    lower = lane < half

    def pack_edges(s):
        for copy in own[s]:
            copy.wait()
        rows = slice(half, half + side)
        west_src[s] = jnp.where(
            lower, pads[s][1, 0, rows], pltpu.roll(pads[s][1, 1, rows], half, 1)
        )
        east_src[s] = jnp.where(
            lower, pltpu.roll(pads[s][2, 1, rows], half, 1), pads[s][2, 0, rows]
        )

    pack_edges(0)
    pl.semaphore_wait(barrier, expected)
    send_all(lambda d: halo_copy(0, d))
    pack_edges(1)
    send_all(lambda d: halo_copy(1, d))

    row_at = [row_ref[j] for j in range(count)]
    col_at = [col_ref[j] for j in range(count)]
    row_grid = lax.broadcasted_iota(jnp.int32, (2 * side, side), 0)
    col_grid = lax.broadcasted_iota(jnp.int32, (2 * side, side), 1)
    place_rows = jnp.concatenate(
        [
            jnp.where(row_grid - col_grid == row_at[j], 1.0, 0.0).astype(bf16)
            for j in range(count)
        ],
        axis=1,
    )

    def lane_mask(j, k):
        offset = lane + (side * k + half) - col_at[j]
        offset = jnp.where(offset < 0, offset + 3 * side, offset)
        offset = jnp.where(offset >= 3 * side, offset - 3 * side, offset)
        return jnp.where(offset < side, 1.0, 0.0).astype(bf16)

    def join_halo(s):
        east, west = east_in[s], west_in[s]
        halo = (
            jnp.where(lower, east, west),
            pltpu.roll(jnp.where(lower, west, east), half, 1),
        )
        for part in range(2):
            pads[s][0, part] = halo[part]
            pads[s][3, part] = halo[part]

    def gather(s, out):
        for j in range(count):
            start = col_at[j] + half
            tile = lax.div(start, side)
            shift = lax.rem(start, side)
            back = lax.rem(side - shift, side)
            for part in range(2):
                near = pads[s][tile, part, pl.ds(row_at[j], side)]
                far = pads[s][tile + 1, part, pl.ds(row_at[j], side)]
                out[j * side : (j + 1) * side, part * side : (part + 1) * side] = pltpu.roll(
                    jnp.where(lane >= shift, near, far), back, 1
                )

    def by_rows(values, inverse=False):
        k = 2 if inverse else 0
        high, low = split(values)
        return dot(high, tab[k]) + dot(low, tab[k]) + dot(high, tab[k + 1])

    def by_cols(values, inverse=False):
        k = 0 if inverse else 2
        high, low = split(values)
        return dot(tab[k], high) + dot(tab[k], low) + dot(tab[k + 1], high)

    def stand(values):
        return jnp.concatenate(
            [
                jnp.concatenate(
                    [
                        values[j * side : (j + 1) * side, part * side : (part + 1) * side]
                        for j in range(count)
                    ],
                    axis=1,
                )
                for part in range(2)
            ],
            axis=0,
        )

    def lie(values):
        return jnp.concatenate(
            [
                jnp.concatenate(
                    [
                        values[part * side : (part + 1) * side, j * side : (j + 1) * side]
                        for part in range(2)
                    ],
                    axis=1,
                )
                for j in range(count)
            ],
            axis=0,
        )

    def real(values):
        return values[:, :side]

    def imag(values):
        return values[:, side:]

    def times(left, right):
        return jnp.concatenate(
            [
                real(left) * real(right) - imag(left) * imag(right),
                real(left) * imag(right) + imag(left) * real(right),
            ],
            axis=1,
        )

    def conj_times(left, right):
        return jnp.concatenate(
            [
                real(left) * real(right) + imag(left) * imag(right),
                real(left) * imag(right) - imag(left) * real(right),
            ],
            axis=1,
        )

    def propagate(values, sign):
        spectrum = by_cols(stand(by_rows(values)))
        h_real = jnp.concatenate([fres[0]] * count, axis=1)
        h_imag = jnp.concatenate([fres[1]] * count, axis=1) * sign
        s_real, s_imag = spectrum[:side], spectrum[side:]
        spectrum = jnp.concatenate(
            [s_real * h_real - s_imag * h_imag, s_real * h_imag + s_imag * h_real], axis=0
        )
        return by_rows(lie(by_cols(spectrum, True)), True)

    def place(s, values):
        pieces = ([], [])
        for j in range(count):
            start = lax.rem(col_at[j] + half, side)
            masks = [lane_mask(j, k) for k in range(3)]
            for part in range(2):
                window = values[j * side : (j + 1) * side, part * side : (part + 1) * side]
                for piece, block in zip(pieces, split(pltpu.roll(window, start, 1))):
                    piece.append(jnp.concatenate([block * m for m in masks], axis=1))
        total = None
        for piece in pieces:
            both = jnp.concatenate(
                [
                    jnp.concatenate([piece[2 * j], piece[2 * j + 1]], axis=1)
                    for j in range(count)
                ],
                axis=0,
            )
            part_sum = dot(place_rows, both)
            total = part_sum if total is None else total + part_sum
        accs[s][0] = total[:, : 3 * side]
        accs[s][1] = total[:, 3 * side :]
        halo_real, halo_imag = total[:, 2 * side : 3 * side], total[:, 5 * side :]
        turned = pltpu.roll(halo_imag, half, 1)
        fe_src[s] = jnp.where(lower, halo_real, turned)
        fw_src[s] = jnp.where(lower, turned, halo_real)

    def finish(s):
        from_west = fw_in[s, 0:side] + fw_in[s, side : 2 * side]
        from_east = fe_in[s, 0:side] + fe_in[s, side : 2 * side]
        for part in range(2):
            if part:
                from_west = pltpu.roll(from_west, half, 1)
                from_east = pltpu.roll(from_east, half, 1)
            rows = slice(half, half + side)
            above_below = jnp.concatenate([ns_in[s, 0, part], ns_in[s, 1, part]], axis=0)
            og[s, part, :, 0:side] = (
                accs[s][part, rows, 0:side]
                + above_below[:, 0:side]
                + jnp.where(lower, from_west, 0.0)
            )
            og[s, part, :, side:tile_w] = (
                accs[s][part, rows, side:tile_w]
                + above_below[:, side:tile_w]
                + jnp.where(lower, 0.0, from_east)
            )
        out_copy(s).start()

    def out_copy(s):
        return pltpu.make_async_copy(og.at[s], og_ref.at[s], local_sem.at[s])

    for copy in loads[:3]:
        copy.wait()
    illumination = jnp.concatenate([ill[0], ill[1]], axis=1)
    probe = jnp.concatenate([illumination] * count, axis=0)

    receive_all(lambda d: halo_copy(0, d))
    join_halo(0)
    gather(0, first_w)
    moved_s[...] = propagate(times(probe, first_w[...]), 1.0)

    receive_all(lambda d: halo_copy(1, d))
    join_halo(1)
    gather(1, second_w)
    far = by_cols(stand(by_rows(times(moved_s[...], second_w[...]))))
    loads[3].wait()
    measured = jnp.concatenate([inten[j] for j in range(count)], axis=1)
    far_real, far_imag = far[:side], far[side:]
    residual = far_real * far_real + far_imag * far_imag - measured
    far_grad = jnp.concatenate([far_real * residual, far_imag * residual], axis=0)
    exit_grad = by_rows(lie(by_cols(far_grad, True)), True)

    place(1, conj_times(moved_s[...], exit_grad))
    send_all(lambda d: fold_copy(1, d))

    entry_grad = propagate(conj_times(second_w[...], exit_grad), -1.0)
    probe_local = conj_times(first_w[...], entry_grad)
    probe_local = sum(probe_local[j * side : (j + 1) * side] for j in range(count))
    ar_src[0:side] = real(probe_local)
    ar_src[side : 2 * side] = imag(probe_local)

    chunk = 2 * side // inner

    def rows_of(number):
        return pl.ds(pl.multiple_of(number * chunk, chunk), chunk)

    def scatter_copy(k):
        number, device = inner_device(k)
        return pltpu.make_async_remote_copy(
            src_ref=ar_src.at[rows_of(number)],
            dst_ref=ar_in.at[rows_of(my_inner)],
            send_sem=ar_send.at[0],
            recv_sem=ar_recv.at[0],
            device_id=device,
            device_id_type=MESH,
        )

    def outer_copy(k):
        number, device = outer_device(k)
        return pltpu.make_async_remote_copy(
            src_ref=z_in.at[rows_of(my_outer)],
            dst_ref=z_in.at[rows_of(my_outer)],
            send_sem=ar_send.at[1],
            recv_sem=ar_recv.at[1],
            device_id=device,
            device_id_type=MESH,
        )

    def gather_copy(k):
        number, device = inner_device(k)
        return pltpu.make_async_remote_copy(
            src_ref=ar_out.at[rows_of(my_inner)],
            dst_ref=ar_out.at[rows_of(my_inner)],
            send_sem=ar_send.at[2],
            recv_sem=ar_recv.at[2],
            device_id=device,
            device_id_type=MESH,
        )

    def start_many(copy_of, number):
        def step(k, carry):
            copy_of(k).start()
            return carry

        lax.fori_loop(1, number, step, 0)

    def wait_many(buffer, number, sem):
        part = buffer.at[0 : (number - 1) * chunk]
        pltpu.make_async_copy(part, part, sem).wait()

    start_many(scatter_copy, inner)
    place(0, conj_times(probe, entry_grad))
    send_all(lambda d: fold_copy(0, d))

    ar_in[rows_of(my_inner)] = ar_src[rows_of(my_inner)]
    wait_many(ar_in, inner, ar_recv.at[0])
    z_in[rows_of(my_outer)] = sum(ar_in[k * chunk : (k + 1) * chunk] for k in range(inner))
    start_many(outer_copy, outer)

    receive_all(lambda d: fold_copy(1, d))
    finish(1)

    wait_many(z_in, outer, ar_recv.at[1])
    positions = count * n_row * n_col
    ar_out[rows_of(my_inner)] = sum(z_in[k * chunk : (k + 1) * chunk] for k in range(outer)) * (
        1.0 / math.sqrt(positions)
    )
    start_many(gather_copy, inner)

    receive_all(lambda d: fold_copy(0, d))
    finish(0)

    wait_many(ar_out, inner, ar_recv.at[2])
    probe_copies = [
        pltpu.make_async_copy(
            ar_out.at[part * side : (part + 1) * side], pg_ref.at[part], local_sem.at[2 + part]
        )
        for part in range(2)
    ]
    for copy in probe_copies:
        copy.start()
    wait_many(ar_src, inner, ar_send.at[0])
    wait_many(z_in, outer, ar_send.at[1])
    wait_many(ar_out, inner, ar_send.at[2])
    for s in range(2):
        sent_all(lambda d: halo_copy(s, d))
        sent_all(lambda d: fold_copy(s, d))
        out_copy(s).wait()
    for copy in probe_copies:
        copy.wait()


def on_device(mesh_shape, table, fresnel, objects, illumination, intensity, row_offset, col_offset):
    n_row, n_col = mesh_shape
    outer = (n_row // plane_rows) * (n_col // plane_cols)
    chunk = 2 * side // (plane_rows * plane_cols)
    scratch = [
        (4, 2, 2 * side, side),
        (4, 2, 2 * side, side),
        (2, side, side),
        (2, side, side),
        (2, 2 * side, side),
        (2, 2 * side, side),
        (2, side, side),
        (count, side, side),
        None,
        (2, side, side),
        (count * side, 2 * side),
        (count * side, 2 * side),
        (count * side, 2 * side),
        (2, 2 * side, 3 * side),
        (2, 2 * side, 3 * side),
        (2, 2 * side, side),
        (2, 2 * side, side),
        (2, 2, 2, half, tile_w),
        (2, 2 * side, side),
        (2, 2 * side, side),
        (2, 2, side, tile_w),
        (2 * side, side),
        (2 * side, side),
        (outer * chunk, side),
        (2 * side, side),
    ]
    scratch = [
        pltpu.VMEM((4, 2 * side, 2 * side), bf16) if shape is None else pltpu.VMEM(shape, f32)
        for shape in scratch
    ]
    dma = pltpu.SemaphoreType.DMA
    scratch += [dma((8,)), dma((2, 8)), dma((2, 8)), dma((2, 8)), dma((2, 8)), dma((3,)), dma((3,))]
    smem = pl.BlockSpec(memory_space=pltpu.SMEM)
    anywhere = pl.BlockSpec(memory_space=pl.ANY)
    return pl.pallas_call(
        functools.partial(kernel, mesh_shape),
        out_shape=(
            jax.ShapeDtypeStruct(objects.shape, f32),
            jax.ShapeDtypeStruct(illumination.shape, f32),
        ),
        in_specs=[smem, smem] + [anywhere] * 5,
        out_specs=(anywhere, anywhere),
        scratch_shapes=scratch,
        compiler_params=pltpu.CompilerParams(
            collective_id=0, has_side_effects=True, vmem_limit_bytes=48 * 1024 * 1024
        ),
        name="ptychography",
    )(row_offset, col_offset, objects, illumination, intensity, table, fresnel)


def solution(mesh):
    table, fresnel = tables()
    shape = (mesh.shape["row"], mesh.shape["col"])

    def whole(objects, illumination, intensity, row_offset, col_offset):
        return jax.shard_map(
            functools.partial(on_device, shape),
            mesh=mesh,
            in_specs=(
                P(),
                P(),
                P(None, None, "row", "col"),
                P(),
                P(("row", "col"), None, None),
                P(("row", "col")),
                P(("row", "col")),
            ),
            out_specs=(P(None, None, "row", "col"), P()),
            check_vma=False,
        )(jnp.asarray(table), jnp.asarray(fresnel), objects, illumination, intensity, row_offset, col_offset)

    return whole
```

```python
import functools
import math

import jax
import jax.numpy as jnp
import ml_dtypes
import numpy as np
from jax import lax
from jax.experimental import pallas as pl
from jax.experimental.pallas import tpu as pltpu
from jax.sharding import PartitionSpec as P

depth = 0.5
side = 128
half = 64
tile_w = 256
count = 4
plane_rows = 8
direct = 40
rest = half - direct
plane_cols = 4
directions = ((-1, 0), (1, 0), (0, -1), (0, 1), (-1, -1), (-1, 1), (1, -1), (1, 1))
MESH = pl.DeviceIdType.MESH
f32 = jnp.float32
bf16 = jnp.bfloat16


def in_two(values):
    high = values.astype(ml_dtypes.bfloat16)
    low = (values - high.astype(np.float64)).astype(ml_dtypes.bfloat16)
    return high, low


def tables():
    index = np.arange(side)
    angle = -2.0 * math.pi / side * (index[:, None] * index[None, :] % side)
    real, imag = np.cos(angle) / math.sqrt(side), np.sin(angle) / math.sqrt(side)
    rows = np.block([[real, imag], [-imag, real]])
    cols = np.block([[real, -imag], [imag, real]])
    signed = np.where(index < side // 2, index, index - side)
    square = signed[:, None] ** 2 + signed[None, :] ** 2
    phase = -math.pi * depth / side * square
    fresnel = np.stack([np.cos(phase), np.sin(phase)]).astype(np.float32)
    return np.stack(in_two(rows) + in_two(cols)), fresnel


def split(values):
    high = values.astype(bf16)
    return high, (values - high.astype(f32)).astype(bf16)


def dot(left, right):
    return lax.dot_general(left, right, (((1,), (0,)), ((), ())), preferred_element_type=f32)


def kernel(
    mesh_shape,
    row_ref,
    col_ref,
    obj_ref,
    ill_ref,
    int_ref,
    tab_ref,
    fres_ref,
    og_ref,
    pg_ref,
    pad0,
    pad1,
    east_src,
    west_src,
    east_in,
    west_in,
    ill,
    inten,
    tab,
    fres,
    first_w,
    second_w,
    moved_s,
    acc0,
    acc1,
    fe_src,
    fw_src,
    ns_in,
    fe_in,
    fw_in,
    og,
    ar_src,
    ar_in,
    z_in,
    ar_out,
    relay_corner,
    relay_rest,
    local_sem,
    msg_send,
    msg_recv,
    relay_send,
    relay_recv,
    ar_send,
    ar_recv,
):
    n_row, n_col = mesh_shape
    row, col = lax.axis_index("row"), lax.axis_index("col")
    pads, accs = (pad0, pad1), (acc0, acc1)

    own = [
        [
            pltpu.make_async_copy(
                obj_ref.at[s, :, :, t * side : (t + 1) * side],
                pads[s].at[t + 1, :, half : half + side],
                local_sem.at[2 * s + t],
            )
            for t in range(2)
        ]
        for s in range(2)
    ]
    loads = [
        pltpu.make_async_copy(ill_ref, ill, local_sem.at[4]),
        pltpu.make_async_copy(tab_ref, tab, local_sem.at[5]),
        pltpu.make_async_copy(fres_ref, fres, local_sem.at[6]),
        pltpu.make_async_copy(int_ref, inten, local_sem.at[7]),
    ]
    for copy in own[0] + own[1] + loads:
        copy.start()

    messages = [(d, 0, half if d[1] else direct) for d in directions]
    messages += [((-1, 0), direct, rest), ((1, 0), direct, rest)]

    def halo_dst(s, m):
        (dr, dc), first, size = messages[m]
        if dc == 0:
            start = first + (3 * half if dr < 0 else 0)
            return pads[s].at[1:3, :, start : start + size]
        into = west_in if dc > 0 else east_in
        start, size = ((half, side) if dr == 0 else (3 * half, half) if dr < 0 else (0, half))
        return into.at[s, start : start + size]

    def halo_src(s, m):
        (dr, dc), first, size = messages[m]
        if dc == 0:
            start = first + (half if dr < 0 else side)
            return pads[s].at[1:3, :, start : start + size]
        start, size = ((0, side) if dr == 0 else (0, half) if dr < 0 else (half, half))
        return (east_src if dc > 0 else west_src).at[s, start : start + size]

    def fold_dst(s, m):
        (dr, dc), first, size = messages[m]
        if dc == 0:
            return ns_in.at[s, 1 if dr < 0 else 0, :, :, first : first + size]
        into = fw_in if dc > 0 else fe_in
        start, size = ((0, side) if dr == 0 else (3 * half, half) if dr < 0 else (side, half))
        return into.at[s, start : start + size]

    def fold_src(s, m):
        (dr, dc), first, size = messages[m]
        if dc == 0:
            start = first + (0 if dr < 0 else 3 * half)
            return accs[s].at[0:2, :, start : start + size]
        start, size = ((half, side) if dr == 0 else (0, half) if dr < 0 else (3 * half, half))
        return (fe_src if dc > 0 else fw_src).at[s, start : start + size]

    ends = ((halo_src, halo_dst), (fold_src, fold_dst))
    row_in, row_out = lax.rem(row, plane_rows), lax.div(row, plane_rows)
    n_out = n_row // plane_rows

    def has(dr, dc):
        found = None
        if dr:
            found = (row > 0) if dr < 0 else (row < n_row - 1)
        if dc:
            col_found = (col > 0) if dc < 0 else (col < n_col - 1)
            found = col_found if found is None else jnp.logical_and(found, col_found)
        return found

    def also(*flags):
        return functools.reduce(jnp.logical_and, [flag for flag in flags if flag is not None])

    def relayed(m):
        (dr, dc), first, _ = messages[m]
        return dr != 0 and (dc != 0 or first != 0)

    def relay_at(m):
        (dr, dc), _, _ = messages[m]
        number = 2 if dc == 0 else 1 if dc > 0 else 0
        return 2 * number + (1 if dr > 0 else 2)

    def sends(m):
        return has(*messages[m][0])

    def receives(m):
        dr, dc = messages[m][0]
        return has(-dr, -dc)

    def leaves_group(m):
        return row_in == (plane_rows - 1 if messages[m][0][0] > 0 else 0)

    def enters_group(m):
        return row_in == (0 if messages[m][0][0] > 0 else plane_rows - 1)

    def relays(m):
        dr, dc = messages[m][0]
        group = (row_out > 0) if dr < 0 else (row_out < n_out - 1)
        return also(row_in == relay_at(m), group, has(0, dc) if dc else None)

    def relay_row(m):
        dr = messages[m][0][0]
        return row + 1 - plane_rows + relay_at(m) if dr > 0 else row + relay_at(m)

    def target_of_relay(m):
        dr, dc = messages[m][0]
        return row - relay_at(m) + (plane_rows if dr > 0 else -1), col + dc

    def relay_buffer(phase, s, m):
        return (relay_rest if messages[m][0][1] == 0 else relay_corner).at[phase, s]

    def remote(src, dst, send, recv, device):
        return pltpu.make_async_remote_copy(
            src_ref=src,
            dst_ref=dst,
            send_sem=send,
            recv_sem=recv,
            device_id=device,
            device_id_type=MESH,
        )

    def straight(phase, s, m):
        src, dst = ends[phase]
        dr, dc = messages[m][0]
        return remote(
            src(s, m),
            dst(s, m),
            msg_send.at[phase, s, m],
            msg_recv.at[phase, s, m],
            (row + dr, col + dc),
        )

    def to_relay(phase, s, m):
        return remote(
            ends[phase][0](s, m),
            relay_buffer(phase, s, m),
            msg_send.at[phase, s, m],
            relay_recv.at[phase, s],
            (relay_row(m), col),
        )

    def from_relay(phase, s, m):
        return remote(
            relay_buffer(phase, s, m),
            ends[phase][1](s, m),
            relay_send.at[phase, s],
            msg_recv.at[phase, s, m],
            target_of_relay(m),
        )

    for m in range(len(messages)):

        @pl.when(jnp.logical_not(receives(m)))
        def _(m=m):
            for s in range(2):
                for dst in (halo_dst(s, m), fold_dst(s, m)):
                    dst[...] = jnp.zeros(dst.shape, f32)

    inner, outer = plane_rows * plane_cols, (n_row // plane_rows) * (n_col // plane_cols)
    outer_cols = n_col // plane_cols
    col_in, col_out = lax.rem(col, plane_cols), lax.div(col, plane_cols)
    my_inner = row_in * plane_cols + col_in
    my_outer = row_out * outer_cols + col_out

    def inner_device(k):
        number = lax.rem(my_inner + k, inner)
        return number, (
            row_out * plane_rows + lax.div(number, plane_cols),
            col_out * plane_cols + lax.rem(number, plane_cols),
        )

    def outer_device(k):
        number = lax.rem(my_outer + k, outer)
        return number, (
            lax.div(number, outer_cols) * plane_rows + row_in,
            lax.rem(number, outer_cols) * plane_cols + col_in,
        )

    barrier = pltpu.get_barrier_semaphore()
    expected = jnp.int32(inner + outer - 2)

    def greet_if(flag, device):
        @pl.when(flag)
        def _():
            pl.semaphore_signal(barrier, inc=1, device_id=device, device_id_type=MESH)

    for m in range(len(messages)):
        dr, dc = messages[m][0]
        expected = expected + sends(m).astype(jnp.int32)
        if relayed(m):
            expected = expected + relays(m).astype(jnp.int32)
            greet_if(
                also(receives(m), jnp.logical_not(enters_group(m))), (row - dr, col - dc)
            )
            greet_if(
                also(receives(m), enters_group(m)),
                (row + relay_at(m) + (-plane_rows if dr > 0 else 1), col - dc),
            )
            greet_if(
                relays(m),
                (row - relay_at(m) + (plane_rows - 1 if dr > 0 else 0), col),
            )
        else:
            greet_if(receives(m), (row - dr, col - dc))

    def greet(device_of):
        def step(k, carry):
            pl.semaphore_signal(barrier, inc=1, device_id=device_of(k)[1], device_id_type=MESH)
            return carry

        return step

    lax.fori_loop(1, inner, greet(inner_device), 0)
    lax.fori_loop(1, outer, greet(outer_device), 0)

    def each(phase, s, straight_do, relay_do=None):
        for m in range(len(messages)):
            if relayed(m):
                flag = also(sends(m), jnp.logical_not(leaves_group(m)))

                @pl.when(also(sends(m), leaves_group(m)))
                def _(m=m):
                    straight_do(to_relay(phase, s, m))

            else:
                flag = sends(m)

            @pl.when(flag)
            def _(m=m):
                straight_do(straight(phase, s, m))

            if relay_do is not None and relayed(m):

                @pl.when(relays(m))
                def _(m=m):
                    relay_do(from_relay(phase, s, m))

    def send_all(phase, s):
        each(phase, s, lambda copy: copy.start())

    def pass_on(phase, s):
        for m in range(len(messages)):
            if relayed(m):

                @pl.when(relays(m))
                def _(m=m):
                    to_relay(phase, s, m).wait_recv()
                    from_relay(phase, s, m).start()

    def receive_all(phase, s):
        for m in range(len(messages)):

            @pl.when(receives(m))
            def _(m=m):
                straight(phase, s, m).wait_recv()

    def sent_all(phase, s):
        each(phase, s, lambda copy: copy.wait_send(), lambda copy: copy.wait_send())

    lane = lax.broadcasted_iota(jnp.int32, (1, side), 1)
    lower = lane < half

    def pack_edges(s):
        for copy in own[s]:
            copy.wait()
        rows = slice(half, half + side)
        west_src[s] = jnp.where(
            lower, pads[s][1, 0, rows], pltpu.roll(pads[s][1, 1, rows], half, 1)
        )
        east_src[s] = jnp.where(
            lower, pltpu.roll(pads[s][2, 1, rows], half, 1), pads[s][2, 0, rows]
        )

    pack_edges(0)
    pl.semaphore_wait(barrier, expected)
    send_all(0, 0)
    pack_edges(1)
    send_all(0, 1)

    row_at = [row_ref[j] for j in range(count)]
    col_at = [col_ref[j] for j in range(count)]
    row_grid = lax.broadcasted_iota(jnp.int32, (2 * side, side), 0)
    col_grid = lax.broadcasted_iota(jnp.int32, (2 * side, side), 1)
    place_rows = jnp.concatenate(
        [
            jnp.where(row_grid - col_grid == row_at[j], 1.0, 0.0).astype(bf16)
            for j in range(count)
        ],
        axis=1,
    )

    def lane_mask(j, k):
        offset = lane + (side * k + half) - col_at[j]
        offset = jnp.where(offset < 0, offset + 3 * side, offset)
        offset = jnp.where(offset >= 3 * side, offset - 3 * side, offset)
        return jnp.where(offset < side, 1.0, 0.0).astype(bf16)

    def join_halo(s):
        east, west = east_in[s], west_in[s]
        halo = (
            jnp.where(lower, east, west),
            pltpu.roll(jnp.where(lower, west, east), half, 1),
        )
        for part in range(2):
            pads[s][0, part] = halo[part]
            pads[s][3, part] = halo[part]

    def gather(s, out):
        for j in range(count):
            start = col_at[j] + half
            tile = lax.div(start, side)
            shift = lax.rem(start, side)
            back = lax.rem(side - shift, side)
            for part in range(2):
                near = pads[s][tile, part, pl.ds(row_at[j], side)]
                far = pads[s][tile + 1, part, pl.ds(row_at[j], side)]
                out[j * side : (j + 1) * side, part * side : (part + 1) * side] = pltpu.roll(
                    jnp.where(lane >= shift, near, far), back, 1
                )

    def by_rows(values, inverse=False):
        k = 2 if inverse else 0
        high, low = split(values)
        return dot(high, tab[k]) + dot(low, tab[k]) + dot(high, tab[k + 1])

    def by_cols(values, inverse=False):
        k = 0 if inverse else 2
        high, low = split(values)
        return dot(tab[k], high) + dot(tab[k], low) + dot(tab[k + 1], high)

    def stand(values):
        return jnp.concatenate(
            [
                jnp.concatenate(
                    [
                        values[j * side : (j + 1) * side, part * side : (part + 1) * side]
                        for j in range(count)
                    ],
                    axis=1,
                )
                for part in range(2)
            ],
            axis=0,
        )

    def lie(values):
        return jnp.concatenate(
            [
                jnp.concatenate(
                    [
                        values[part * side : (part + 1) * side, j * side : (j + 1) * side]
                        for part in range(2)
                    ],
                    axis=1,
                )
                for j in range(count)
            ],
            axis=0,
        )

    def real(values):
        return values[:, :side]

    def imag(values):
        return values[:, side:]

    def times(left, right):
        return jnp.concatenate(
            [
                real(left) * real(right) - imag(left) * imag(right),
                real(left) * imag(right) + imag(left) * real(right),
            ],
            axis=1,
        )

    def conj_times(left, right):
        return jnp.concatenate(
            [
                real(left) * real(right) + imag(left) * imag(right),
                real(left) * imag(right) - imag(left) * real(right),
            ],
            axis=1,
        )

    def propagate(values, sign):
        spectrum = by_cols(stand(by_rows(values)))
        h_real = jnp.concatenate([fres[0]] * count, axis=1)
        h_imag = jnp.concatenate([fres[1]] * count, axis=1) * sign
        s_real, s_imag = spectrum[:side], spectrum[side:]
        spectrum = jnp.concatenate(
            [s_real * h_real - s_imag * h_imag, s_real * h_imag + s_imag * h_real], axis=0
        )
        return by_rows(lie(by_cols(spectrum, True)), True)

    def place(s, values):
        pieces = ([], [])
        for j in range(count):
            start = lax.rem(col_at[j] + half, side)
            masks = [lane_mask(j, k) for k in range(3)]
            for part in range(2):
                window = values[j * side : (j + 1) * side, part * side : (part + 1) * side]
                for piece, block in zip(pieces, split(pltpu.roll(window, start, 1))):
                    piece.append(jnp.concatenate([block * m for m in masks], axis=1))
        total = None
        for piece in pieces:
            both = jnp.concatenate(
                [
                    jnp.concatenate([piece[2 * j], piece[2 * j + 1]], axis=1)
                    for j in range(count)
                ],
                axis=0,
            )
            part_sum = dot(place_rows, both)
            total = part_sum if total is None else total + part_sum
        for part in range(2):
            for tile in range(3):
                start = (3 * part + tile) * side
                accs[s][tile, part] = total[:, start : start + side]
        halo_real, halo_imag = total[:, 2 * side : 3 * side], total[:, 5 * side :]
        turned = pltpu.roll(halo_imag, half, 1)
        fe_src[s] = jnp.where(lower, halo_real, turned)
        fw_src[s] = jnp.where(lower, turned, halo_real)

    def finish(s):
        from_west = fw_in[s, 0:side] + fw_in[s, side : 2 * side]
        from_east = fe_in[s, 0:side] + fe_in[s, side : 2 * side]
        for part in range(2):
            if part:
                from_west = pltpu.roll(from_west, half, 1)
                from_east = pltpu.roll(from_east, half, 1)
            rows = slice(half, half + side)
            for tile in range(2):
                beside = jnp.where(lower == (tile == 0), from_east if tile else from_west, 0.0)
                above_below = jnp.concatenate(
                    [ns_in[s, 0, tile, part], ns_in[s, 1, tile, part]], axis=0
                )
                og[s, part, :, tile * side : (tile + 1) * side] = (
                    accs[s][tile, part, rows] + above_below + beside
                )
        out_copy(s).start()

    def out_copy(s):
        return pltpu.make_async_copy(og.at[s], og_ref.at[s], local_sem.at[s])

    for copy in loads[:3]:
        copy.wait()
    illumination = jnp.concatenate([ill[0], ill[1]], axis=1)
    probe = jnp.concatenate([illumination] * count, axis=0)

    pass_on(0, 0)
    receive_all(0, 0)
    join_halo(0)
    gather(0, first_w)
    pass_on(0, 1)
    moved_s[...] = propagate(times(probe, first_w[...]), 1.0)

    receive_all(0, 1)
    join_halo(1)
    gather(1, second_w)
    far = by_cols(stand(by_rows(times(moved_s[...], second_w[...]))))
    loads[3].wait()
    measured = jnp.concatenate([inten[j] for j in range(count)], axis=1)
    far_real, far_imag = far[:side], far[side:]
    residual = far_real * far_real + far_imag * far_imag - measured
    far_grad = jnp.concatenate([far_real * residual, far_imag * residual], axis=0)
    exit_grad = by_rows(lie(by_cols(far_grad, True)), True)

    place(1, conj_times(moved_s[...], exit_grad))
    send_all(1, 1)

    entry_grad = propagate(conj_times(second_w[...], exit_grad), -1.0)
    probe_local = conj_times(first_w[...], entry_grad)
    probe_local = sum(probe_local[j * side : (j + 1) * side] for j in range(count))
    ar_src[0:side] = real(probe_local)
    ar_src[side : 2 * side] = imag(probe_local)

    chunk = 2 * side // inner

    def rows_of(number):
        return pl.ds(pl.multiple_of(number * chunk, chunk), chunk)

    def scatter_copy(k):
        number, device = inner_device(k)
        return pltpu.make_async_remote_copy(
            src_ref=ar_src.at[rows_of(number)],
            dst_ref=ar_in.at[rows_of(my_inner)],
            send_sem=ar_send.at[0],
            recv_sem=ar_recv.at[0],
            device_id=device,
            device_id_type=MESH,
        )

    def outer_copy(k):
        number, device = outer_device(k)
        return pltpu.make_async_remote_copy(
            src_ref=z_in.at[rows_of(my_outer)],
            dst_ref=z_in.at[rows_of(my_outer)],
            send_sem=ar_send.at[1],
            recv_sem=ar_recv.at[1],
            device_id=device,
            device_id_type=MESH,
        )

    def gather_copy(k):
        number, device = inner_device(k)
        return pltpu.make_async_remote_copy(
            src_ref=ar_out.at[rows_of(my_inner)],
            dst_ref=ar_out.at[rows_of(my_inner)],
            send_sem=ar_send.at[2],
            recv_sem=ar_recv.at[2],
            device_id=device,
            device_id_type=MESH,
        )

    def start_many(copy_of, number):
        def step(k, carry):
            copy_of(k).start()
            return carry

        lax.fori_loop(1, number, step, 0)

    def wait_many(buffer, number, sem):
        if number == 1:
            return
        part = buffer.at[0 : (number - 1) * chunk]
        pltpu.make_async_copy(part, part, sem).wait()

    start_many(scatter_copy, inner)
    place(0, conj_times(probe, entry_grad))
    send_all(1, 0)

    ar_in[rows_of(my_inner)] = ar_src[rows_of(my_inner)]
    wait_many(ar_in, inner, ar_recv.at[0])
    z_in[rows_of(my_outer)] = sum(ar_in[k * chunk : (k + 1) * chunk] for k in range(inner))
    start_many(outer_copy, outer)

    pass_on(1, 1)
    receive_all(1, 1)
    finish(1)

    wait_many(z_in, outer, ar_recv.at[1])
    positions = count * n_row * n_col
    ar_out[rows_of(my_inner)] = sum(z_in[k * chunk : (k + 1) * chunk] for k in range(outer)) * (
        1.0 / math.sqrt(positions)
    )
    start_many(gather_copy, inner)

    pass_on(1, 0)
    receive_all(1, 0)
    finish(0)

    wait_many(ar_out, inner, ar_recv.at[2])
    probe_copies = [
        pltpu.make_async_copy(
            ar_out.at[part * side : (part + 1) * side], pg_ref.at[part], local_sem.at[2 + part]
        )
        for part in range(2)
    ]
    for copy in probe_copies:
        copy.start()
    wait_many(ar_src, inner, ar_send.at[0])
    wait_many(z_in, outer, ar_send.at[1])
    wait_many(ar_out, inner, ar_send.at[2])
    for s in range(2):
        sent_all(0, s)
        sent_all(1, s)
        out_copy(s).wait()
    for copy in probe_copies:
        copy.wait()


def on_device(mesh_shape, table, fresnel, objects, illumination, intensity, row_offset, col_offset):
    n_row, n_col = mesh_shape
    outer = (n_row // plane_rows) * (n_col // plane_cols)
    chunk = 2 * side // (plane_rows * plane_cols)
    scratch = [
        (4, 2, 2 * side, side),
        (4, 2, 2 * side, side),
        (2, side, side),
        (2, side, side),
        (2, 2 * side, side),
        (2, 2 * side, side),
        (2, side, side),
        (count, side, side),
        None,
        (2, side, side),
        (count * side, 2 * side),
        (count * side, 2 * side),
        (count * side, 2 * side),
        (3, 2, 2 * side, side),
        (3, 2, 2 * side, side),
        (2, 2 * side, side),
        (2, 2 * side, side),
        (2, 2, 2, 2, half, side),
        (2, 2 * side, side),
        (2, 2 * side, side),
        (2, 2, side, tile_w),
        (2 * side, side),
        (2 * side, side),
        (outer * chunk, side),
        (2 * side, side),
        (2, 2, half, side),
        (2, 2, 2, 2, rest, side),
    ]
    scratch = [
        pltpu.VMEM((4, 2 * side, 2 * side), bf16) if shape is None else pltpu.VMEM(shape, f32)
        for shape in scratch
    ]
    dma = pltpu.SemaphoreType.DMA
    scratch += [dma((8,)), dma((2, 2, 10)), dma((2, 2, 10)), dma((2, 2)), dma((2, 2)), dma((3,)), dma((3,))]
    smem = pl.BlockSpec(memory_space=pltpu.SMEM)
    anywhere = pl.BlockSpec(memory_space=pltpu.HBM)
    return pl.pallas_call(
        functools.partial(kernel, mesh_shape),
        out_shape=(
            jax.ShapeDtypeStruct(objects.shape, f32),
            jax.ShapeDtypeStruct(illumination.shape, f32),
        ),
        in_specs=[smem, smem] + [anywhere] * 5,
        out_specs=(anywhere, anywhere),
        scratch_shapes=scratch,
        compiler_params=pltpu.CompilerParams(
            collective_id=0, has_side_effects=True, vmem_limit_bytes=60 * 1024 * 1024
        ),
        name="ptychography",
    )(row_offset, col_offset, objects, illumination, intensity, table, fresnel)


def solution(mesh):
    table, fresnel = tables()
    shape = (mesh.shape["row"], mesh.shape["col"])

    def whole(objects, illumination, intensity, row_offset, col_offset):
        return jax.shard_map(
            functools.partial(on_device, shape),
            mesh=mesh,
            in_specs=(
                P(),
                P(),
                P(None, None, "row", "col"),
                P(),
                P(("row", "col"), None, None),
                P(("row", "col")),
                P(("row", "col")),
            ),
            out_specs=(P(None, None, "row", "col"), P()),
            check_vma=False,
        )(jnp.asarray(table), jnp.asarray(fresnel), objects, illumination, intensity, row_offset, col_offset)

    return whole
```

```python
import functools
import math

import jax
import jax.numpy as jnp
import ml_dtypes
import numpy as np
from jax import lax
from jax.experimental import pallas as pl
from jax.experimental.pallas import tpu as pltpu
from jax.sharding import PartitionSpec as P

depth = 0.5
side = 128
half = 64
tile_w = 256
count = 4
plane_rows = 8
direct = 40
rest = half - direct
plane_cols = 4
directions = ((-1, 0), (1, 0), (0, -1), (0, 1), (-1, -1), (-1, 1), (1, -1), (1, 1))
MESH = pl.DeviceIdType.MESH
f32 = jnp.float32
bf16 = jnp.bfloat16


def in_two(values):
    high = values.astype(ml_dtypes.bfloat16)
    low = (values - high.astype(np.float64)).astype(ml_dtypes.bfloat16)
    return high, low


def tables():
    index = np.arange(side)
    angle = -2.0 * math.pi / side * (index[:, None] * index[None, :] % side)
    real, imag = np.cos(angle) / math.sqrt(side), np.sin(angle) / math.sqrt(side)
    rows = np.block([[real, imag], [-imag, real]])
    cols = np.block([[real, -imag], [imag, real]])
    signed = np.where(index < side // 2, index, index - side)
    square = signed[:, None] ** 2 + signed[None, :] ** 2
    phase = -math.pi * depth / side * square
    fresnel = np.stack([np.cos(phase), np.sin(phase)]).astype(np.float32)
    return np.stack(in_two(rows) + in_two(cols)), fresnel


def split(values):
    high = values.astype(bf16)
    return high, (values - high.astype(f32)).astype(bf16)


def dot(left, right):
    return lax.dot_general(left, right, (((1,), (0,)), ((), ())), preferred_element_type=f32)


def kernel(
    mesh_shape,
    row_ref,
    col_ref,
    obj_ref,
    ill_ref,
    int_ref,
    tab_ref,
    fres_ref,
    og_ref,
    pg_ref,
    pad0,
    pad1,
    east_src,
    west_src,
    east_in,
    west_in,
    ill,
    inten,
    tab,
    fres,
    first_w,
    second_w,
    moved_s,
    acc0,
    acc1,
    fe_src,
    fw_src,
    ns_in,
    fe_in,
    fw_in,
    og,
    ar_src,
    ar_in,
    z_in,
    ar_out,
    relay_corner,
    relay_rest,
    local_sem,
    msg_send,
    msg_recv,
    relay_send,
    relay_recv,
    ar_send,
    ar_recv,
    stage_sem,
):
    n_row, n_col = mesh_shape
    row, col = lax.axis_index("row"), lax.axis_index("col")
    pads, accs = (pad0, pad1), (acc0, acc1)

    own = [
        [
            pltpu.make_async_copy(
                obj_ref.at[s, :, :, t * side : (t + 1) * side],
                pads[s].at[t + 1, :, half : half + side],
                local_sem.at[2 * s + t],
            )
            for t in range(2)
        ]
        for s in range(2)
    ]
    loads = [
        pltpu.make_async_copy(ill_ref, ill, local_sem.at[4]),
        pltpu.make_async_copy(tab_ref, tab, local_sem.at[5]),
        pltpu.make_async_copy(fres_ref, fres, local_sem.at[6]),
        pltpu.make_async_copy(int_ref, inten, local_sem.at[7]),
    ]
    for copy in own[0] + own[1] + loads:
        copy.start()

    messages = [(d, 0, half if d[1] else direct) for d in directions]
    messages += [((-1, 0), direct, rest), ((1, 0), direct, rest)]

    def halo_dst(s, m):
        (dr, dc), first, size = messages[m]
        if dc == 0:
            start = first + (3 * half if dr < 0 else 0)
            return pads[s].at[1:3, :, start : start + size]
        into = west_in if dc > 0 else east_in
        start, size = ((half, side) if dr == 0 else (3 * half, half) if dr < 0 else (0, half))
        return into.at[s, start : start + size]

    def halo_src(s, m):
        (dr, dc), first, size = messages[m]
        if dc == 0:
            start = first + (half if dr < 0 else side)
            return pads[s].at[1:3, :, start : start + size]
        start, size = ((0, side) if dr == 0 else (0, half) if dr < 0 else (half, half))
        return (east_src if dc > 0 else west_src).at[s, start : start + size]

    def fold_dst(s, m):
        (dr, dc), first, size = messages[m]
        if dc == 0:
            return ns_in.at[s, 1 if dr < 0 else 0, :, :, first : first + size]
        into = fw_in if dc > 0 else fe_in
        start, size = ((0, side) if dr == 0 else (3 * half, half) if dr < 0 else (side, half))
        return into.at[s, start : start + size]

    def fold_src(s, m):
        (dr, dc), first, size = messages[m]
        if dc == 0:
            start = first + (0 if dr < 0 else 3 * half)
            return accs[s].at[0:2, :, start : start + size]
        start, size = ((half, side) if dr == 0 else (0, half) if dr < 0 else (3 * half, half))
        return (fe_src if dc > 0 else fw_src).at[s, start : start + size]

    ends = ((halo_src, halo_dst), (fold_src, fold_dst))
    row_in, row_out = lax.rem(row, plane_rows), lax.div(row, plane_rows)
    n_out = n_row // plane_rows

    def has(dr, dc):
        found = None
        if dr:
            found = (row > 0) if dr < 0 else (row < n_row - 1)
        if dc:
            col_found = (col > 0) if dc < 0 else (col < n_col - 1)
            found = col_found if found is None else jnp.logical_and(found, col_found)
        return found

    def also(*flags):
        return functools.reduce(jnp.logical_and, [flag for flag in flags if flag is not None])

    def relayed(m):
        (dr, dc), first, _ = messages[m]
        return dr != 0 and (dc != 0 or first != 0)

    def relay_at(m):
        (dr, dc), _, _ = messages[m]
        number = 2 if dc == 0 else 1 if dc > 0 else 0
        return 2 * number + (1 if dr > 0 else 2)

    def sends(m):
        return has(*messages[m][0])

    def receives(m):
        dr, dc = messages[m][0]
        return has(-dr, -dc)

    def leaves_group(m):
        return row_in == (plane_rows - 1 if messages[m][0][0] > 0 else 0)

    def enters_group(m):
        return row_in == (0 if messages[m][0][0] > 0 else plane_rows - 1)

    def relays(m):
        dr, dc = messages[m][0]
        group = (row_out > 0) if dr < 0 else (row_out < n_out - 1)
        return also(row_in == relay_at(m), group, has(0, dc) if dc else None)

    def relay_row(m):
        dr = messages[m][0][0]
        return row + 1 - plane_rows + relay_at(m) if dr > 0 else row + relay_at(m)

    def target_of_relay(m):
        dr, dc = messages[m][0]
        return row - relay_at(m) + (plane_rows if dr > 0 else -1), col + dc

    def relay_buffer(phase, s, m):
        return (relay_rest if messages[m][0][1] == 0 else relay_corner).at[phase, s]

    def remote(src, dst, send, recv, device):
        return pltpu.make_async_remote_copy(
            src_ref=src,
            dst_ref=dst,
            send_sem=send,
            recv_sem=recv,
            device_id=device,
            device_id_type=MESH,
        )

    def straight(phase, s, m):
        src, dst = ends[phase]
        dr, dc = messages[m][0]
        return remote(
            src(s, m),
            dst(s, m),
            msg_send.at[phase, s, m],
            msg_recv.at[phase, s, m],
            (row + dr, col + dc),
        )

    def to_relay(phase, s, m):
        return remote(
            ends[phase][0](s, m),
            relay_buffer(phase, s, m),
            msg_send.at[phase, s, m],
            relay_recv.at[phase, s],
            (relay_row(m), col),
        )

    def from_relay(phase, s, m):
        return remote(
            relay_buffer(phase, s, m),
            ends[phase][1](s, m),
            relay_send.at[phase, s],
            msg_recv.at[phase, s, m],
            target_of_relay(m),
        )

    for m in range(len(messages)):

        @pl.when(jnp.logical_not(receives(m)))
        def _(m=m):
            for s in range(2):
                for dst in (halo_dst(s, m), fold_dst(s, m)):
                    dst[...] = jnp.zeros(dst.shape, f32)

    inner, outer = plane_rows * plane_cols, (n_row // plane_rows) * (n_col // plane_cols)
    outer_cols = n_col // plane_cols
    col_in, col_out = lax.rem(col, plane_cols), lax.div(col, plane_cols)
    my_inner = row_in * plane_cols + col_in
    my_outer = row_out * outer_cols + col_out

    def hops(step, size):
        return min(step, size - step)

    core_rows = plane_rows // 2
    inner_steps = [
        (y, core, x) for y in range(core_rows) for core in range(2) for x in range(plane_cols)
    ]
    inner_steps.sort(key=lambda k: -2 * (hops(k[0], core_rows) + hops(k[2], plane_cols)) - k[1])
    outer_steps = sorted(range(1, outer), key=lambda k: -hops(k, outer))

    def inner_device(step):
        y, core, x = step
        row_to = lax.rem(lax.div(row_in, 2) + y, core_rows) * 2 + lax.rem(row_in + core, 2)
        col_to = lax.rem(col_in + x, plane_cols)
        number = row_to * plane_cols + col_to
        return number, (row_out * plane_rows + row_to, col_out * plane_cols + col_to)

    def outer_device(step):
        number = lax.rem(my_outer + step, outer)
        return number, (
            lax.div(number, outer_cols) * plane_rows + row_in,
            lax.rem(number, outer_cols) * plane_cols + col_in,
        )

    barrier = pltpu.get_barrier_semaphore()
    expected = jnp.int32(0)

    def greet_if(flag, device):
        @pl.when(flag)
        def _():
            pl.semaphore_signal(barrier, inc=1, device_id=device, device_id_type=MESH)

    def greet(devices, semaphore):
        for device in devices:
            pl.semaphore_signal(semaphore, inc=1, device_id=device, device_id_type=MESH)

    def turn(index, step, size):
        return index - lax.rem(index, size) + lax.rem(lax.rem(index, size) + step, size)

    def far_row(step):
        return lax.rem(row + step * plane_rows, n_row), col

    def far_col(step):
        return row, lax.rem(col + step * plane_cols, n_col)

    line_far = [far_row(k) for k in sorted({1 % n_out, (n_out - 1) % n_out} - {0})]
    line_near = [far_col(k) for k in range(1, outer_cols)]
    line_x = [(row, turn(col, k, plane_cols)) for k in range(1, plane_cols)]
    line_y = [(turn(row, k, plane_rows), col) for k in range(1, plane_rows)]
    lines = line_far + line_near + line_y + line_x
    expected = expected + len(lines)
    greet(line_far, barrier)
    for m in range(len(messages)):
        dr, dc = messages[m][0]
        expected = expected + sends(m).astype(jnp.int32)
        if relayed(m):
            expected = expected + relays(m).astype(jnp.int32)
            greet_if(
                also(receives(m), jnp.logical_not(enters_group(m))), (row - dr, col - dc)
            )
            greet_if(
                also(receives(m), enters_group(m)),
                (row + relay_at(m) + (-plane_rows if dr > 0 else 1), col - dc),
            )
            greet_if(
                relays(m),
                (row - relay_at(m) + (plane_rows - 1 if dr > 0 else 0), col),
            )
        else:
            greet_if(receives(m), (row - dr, col - dc))
    greet(line_near + line_y + line_x, barrier)

    def second_stage():
        greet(line_far + line_x, stage_sem.at[0])

    def third_stage():
        pl.semaphore_wait(stage_sem.at[0], len(line_far + line_x))
        greet(line_near, stage_sem.at[1])

    def last_stage():
        pl.semaphore_wait(stage_sem.at[1], len(line_near))

    order = sorted(range(len(messages)), key=lambda m: not relayed(m))

    def each(phase, s, straight_do, relay_do=None):
        for m in order:
            if relayed(m):
                flag = also(sends(m), jnp.logical_not(leaves_group(m)))

                @pl.when(also(sends(m), leaves_group(m)))
                def _(m=m):
                    straight_do(to_relay(phase, s, m))

            else:
                flag = sends(m)

            @pl.when(flag)
            def _(m=m):
                straight_do(straight(phase, s, m))

            if relay_do is not None and relayed(m):

                @pl.when(relays(m))
                def _(m=m):
                    relay_do(from_relay(phase, s, m))

    def send_all(phase, s):
        each(phase, s, lambda copy: copy.start())

    def pass_on(phase, s):
        for m in range(len(messages)):
            if relayed(m):

                @pl.when(relays(m))
                def _(m=m):
                    to_relay(phase, s, m).wait_recv()
                    from_relay(phase, s, m).start()

    def receive_all(phase, s):
        for m in range(len(messages)):

            @pl.when(receives(m))
            def _(m=m):
                straight(phase, s, m).wait_recv()

    def sent_all(phase, s):
        each(phase, s, lambda copy: copy.wait_send(), lambda copy: copy.wait_send())

    lane = lax.broadcasted_iota(jnp.int32, (1, side), 1)
    lower = lane < half

    def pack_edges(s):
        for copy in own[s]:
            copy.wait()
        rows = slice(half, half + side)
        west_src[s] = jnp.where(
            lower, pads[s][1, 0, rows], pltpu.roll(pads[s][1, 1, rows], half, 1)
        )
        east_src[s] = jnp.where(
            lower, pltpu.roll(pads[s][2, 1, rows], half, 1), pads[s][2, 0, rows]
        )

    pack_edges(0)
    pl.semaphore_wait(barrier, expected)
    send_all(0, 0)
    second_stage()
    pack_edges(1)
    send_all(0, 1)

    row_at = [row_ref[j] for j in range(count)]
    col_at = [col_ref[j] for j in range(count)]
    row_grid = lax.broadcasted_iota(jnp.int32, (2 * side, side), 0)
    col_grid = lax.broadcasted_iota(jnp.int32, (2 * side, side), 1)
    place_rows = jnp.concatenate(
        [
            jnp.where(row_grid - col_grid == row_at[j], 1.0, 0.0).astype(bf16)
            for j in range(count)
        ],
        axis=1,
    )

    def lane_mask(j, k):
        offset = lane + (side * k + half) - col_at[j]
        offset = jnp.where(offset < 0, offset + 3 * side, offset)
        offset = jnp.where(offset >= 3 * side, offset - 3 * side, offset)
        return jnp.where(offset < side, 1.0, 0.0).astype(bf16)

    def join_halo(s):
        east, west = east_in[s], west_in[s]
        halo = (
            jnp.where(lower, east, west),
            pltpu.roll(jnp.where(lower, west, east), half, 1),
        )
        for part in range(2):
            pads[s][0, part] = halo[part]
            pads[s][3, part] = halo[part]

    def gather(s, out):
        for j in range(count):
            start = col_at[j] + half
            tile = lax.div(start, side)
            shift = lax.rem(start, side)
            back = lax.rem(side - shift, side)
            for part in range(2):
                near = pads[s][tile, part, pl.ds(row_at[j], side)]
                far = pads[s][tile + 1, part, pl.ds(row_at[j], side)]
                out[j * side : (j + 1) * side, part * side : (part + 1) * side] = pltpu.roll(
                    jnp.where(lane >= shift, near, far), back, 1
                )

    def by_rows(values, inverse=False):
        k = 2 if inverse else 0
        high, low = split(values)
        return dot(high, tab[k]) + dot(low, tab[k]) + dot(high, tab[k + 1])

    def by_cols(values, inverse=False):
        k = 0 if inverse else 2
        high, low = split(values)
        return dot(tab[k], high) + dot(tab[k], low) + dot(tab[k + 1], high)

    def stand(values):
        return jnp.concatenate(
            [
                jnp.concatenate(
                    [
                        values[j * side : (j + 1) * side, part * side : (part + 1) * side]
                        for j in range(count)
                    ],
                    axis=1,
                )
                for part in range(2)
            ],
            axis=0,
        )

    def lie(values):
        return jnp.concatenate(
            [
                jnp.concatenate(
                    [
                        values[part * side : (part + 1) * side, j * side : (j + 1) * side]
                        for part in range(2)
                    ],
                    axis=1,
                )
                for j in range(count)
            ],
            axis=0,
        )

    def real(values):
        return values[:, :side]

    def imag(values):
        return values[:, side:]

    def times(left, right):
        return jnp.concatenate(
            [
                real(left) * real(right) - imag(left) * imag(right),
                real(left) * imag(right) + imag(left) * real(right),
            ],
            axis=1,
        )

    def conj_times(left, right):
        return jnp.concatenate(
            [
                real(left) * real(right) + imag(left) * imag(right),
                real(left) * imag(right) - imag(left) * real(right),
            ],
            axis=1,
        )

    def propagate(values, sign):
        spectrum = by_cols(stand(by_rows(values)))
        h_real = jnp.concatenate([fres[0]] * count, axis=1)
        h_imag = jnp.concatenate([fres[1]] * count, axis=1) * sign
        s_real, s_imag = spectrum[:side], spectrum[side:]
        spectrum = jnp.concatenate(
            [s_real * h_real - s_imag * h_imag, s_real * h_imag + s_imag * h_real], axis=0
        )
        return by_rows(lie(by_cols(spectrum, True)), True)

    def place(s, values):
        pieces = ([], [])
        for j in range(count):
            start = lax.rem(col_at[j] + half, side)
            masks = [lane_mask(j, k) for k in range(3)]
            for part in range(2):
                window = values[j * side : (j + 1) * side, part * side : (part + 1) * side]
                for piece, block in zip(pieces, split(pltpu.roll(window, start, 1))):
                    piece.append(jnp.concatenate([block * m for m in masks], axis=1))
        total = None
        for piece in pieces:
            both = jnp.concatenate(
                [
                    jnp.concatenate([piece[2 * j], piece[2 * j + 1]], axis=1)
                    for j in range(count)
                ],
                axis=0,
            )
            part_sum = dot(place_rows, both)
            total = part_sum if total is None else total + part_sum
        for part in range(2):
            for tile in range(3):
                start = (3 * part + tile) * side
                accs[s][tile, part] = total[:, start : start + side]
        halo_real, halo_imag = total[:, 2 * side : 3 * side], total[:, 5 * side :]
        turned = pltpu.roll(halo_imag, half, 1)
        fe_src[s] = jnp.where(lower, halo_real, turned)
        fw_src[s] = jnp.where(lower, turned, halo_real)

    def finish(s):
        from_west = fw_in[s, 0:side] + fw_in[s, side : 2 * side]
        from_east = fe_in[s, 0:side] + fe_in[s, side : 2 * side]
        for part in range(2):
            if part:
                from_west = pltpu.roll(from_west, half, 1)
                from_east = pltpu.roll(from_east, half, 1)
            rows = slice(half, half + side)
            for tile in range(2):
                beside = jnp.where(lower == (tile == 0), from_east if tile else from_west, 0.0)
                above_below = jnp.concatenate(
                    [ns_in[s, 0, tile, part], ns_in[s, 1, tile, part]], axis=0
                )
                og[s, part, :, tile * side : (tile + 1) * side] = (
                    accs[s][tile, part, rows] + above_below + beside
                )
        out_copy(s).start()

    def out_copy(s):
        return pltpu.make_async_copy(og.at[s], og_ref.at[s], local_sem.at[s])

    for copy in loads[:3]:
        copy.wait()
    illumination = jnp.concatenate([ill[0], ill[1]], axis=1)
    probe = jnp.concatenate([illumination] * count, axis=0)

    pass_on(0, 0)
    receive_all(0, 0)
    join_halo(0)
    gather(0, first_w)
    pass_on(0, 1)
    third_stage()
    moved_s[...] = propagate(times(probe, first_w[...]), 1.0)

    receive_all(0, 1)
    join_halo(1)
    gather(1, second_w)
    far = by_cols(stand(by_rows(times(moved_s[...], second_w[...]))))
    loads[3].wait()
    measured = jnp.concatenate([inten[j] for j in range(count)], axis=1)
    far_real, far_imag = far[:side], far[side:]
    residual = far_real * far_real + far_imag * far_imag - measured
    far_grad = jnp.concatenate([far_real * residual, far_imag * residual], axis=0)
    exit_grad = by_rows(lie(by_cols(far_grad, True)), True)


    entry_grad = propagate(conj_times(second_w[...], exit_grad), -1.0)
    probe_local = conj_times(first_w[...], entry_grad)
    probe_local = sum(probe_local[j * side : (j + 1) * side] for j in range(count))
    ar_src[0:side] = real(probe_local)
    ar_src[side : 2 * side] = imag(probe_local)

    chunk = 2 * side // inner

    def rows_of(number):
        return pl.ds(pl.multiple_of(number * chunk, chunk), chunk)

    def scatter_copy(k):
        number, device = inner_device(k)
        return pltpu.make_async_remote_copy(
            src_ref=ar_src.at[rows_of(number)],
            dst_ref=ar_in.at[rows_of(my_inner)],
            send_sem=ar_send.at[0],
            recv_sem=ar_recv.at[0],
            device_id=device,
            device_id_type=MESH,
        )

    def outer_copy(k):
        number, device = outer_device(k)
        return pltpu.make_async_remote_copy(
            src_ref=z_in.at[rows_of(my_outer)],
            dst_ref=z_in.at[rows_of(my_outer)],
            send_sem=ar_send.at[1],
            recv_sem=ar_recv.at[1],
            device_id=device,
            device_id_type=MESH,
        )

    def gather_copy(k):
        number, device = inner_device(k)
        return pltpu.make_async_remote_copy(
            src_ref=ar_out.at[rows_of(my_inner)],
            dst_ref=ar_out.at[rows_of(my_inner)],
            send_sem=ar_send.at[2],
            recv_sem=ar_recv.at[2],
            device_id=device,
            device_id_type=MESH,
        )

    def start_many(copy_of, steps):
        for step in steps:
            copy_of(step).start()

    def wait_many(buffer, number, sem):
        if number == 1:
            return
        part = buffer.at[0 : (number - 1) * chunk]
        pltpu.make_async_copy(part, part, sem).wait()

    start_many(scatter_copy, inner_steps[:-1])
    place(1, conj_times(moved_s[...], exit_grad))
    send_all(1, 1)
    place(0, conj_times(probe, entry_grad))
    send_all(1, 0)

    ar_in[rows_of(my_inner)] = ar_src[rows_of(my_inner)]
    pass_on(1, 1)
    pass_on(1, 0)
    wait_many(ar_in, inner, ar_recv.at[0])
    z_in[rows_of(my_outer)] = sum(ar_in[k * chunk : (k + 1) * chunk] for k in range(inner))
    last_stage()
    start_many(outer_copy, outer_steps)


    wait_many(z_in, outer, ar_recv.at[1])
    positions = count * n_row * n_col
    ar_out[rows_of(my_inner)] = sum(z_in[k * chunk : (k + 1) * chunk] for k in range(outer)) * (
        1.0 / math.sqrt(positions)
    )
    start_many(gather_copy, inner_steps[:-1])

    receive_all(1, 1)
    finish(1)
    receive_all(1, 0)
    finish(0)

    wait_many(ar_out, inner, ar_recv.at[2])
    probe_copies = [
        pltpu.make_async_copy(
            ar_out.at[part * side : (part + 1) * side], pg_ref.at[part], local_sem.at[2 + part]
        )
        for part in range(2)
    ]
    for copy in probe_copies:
        copy.start()
    wait_many(ar_src, inner, ar_send.at[0])
    wait_many(z_in, outer, ar_send.at[1])
    wait_many(ar_out, inner, ar_send.at[2])
    for s in range(2):
        sent_all(0, s)
        sent_all(1, s)
        out_copy(s).wait()
    for copy in probe_copies:
        copy.wait()


def in_hbm(x):
    return pltpu.with_memory_space_constraint(x, pltpu.HBM)


def on_device(mesh_shape, table, fresnel, objects, illumination, intensity, row_offset, col_offset):
    n_row, n_col = mesh_shape
    outer = (n_row // plane_rows) * (n_col // plane_cols)
    chunk = 2 * side // (plane_rows * plane_cols)
    scratch = [
        (4, 2, 2 * side, side),
        (4, 2, 2 * side, side),
        (2, side, side),
        (2, side, side),
        (2, 2 * side, side),
        (2, 2 * side, side),
        (2, side, side),
        (count, side, side),
        None,
        (2, side, side),
        (count * side, 2 * side),
        (count * side, 2 * side),
        (count * side, 2 * side),
        (3, 2, 2 * side, side),
        (3, 2, 2 * side, side),
        (2, 2 * side, side),
        (2, 2 * side, side),
        (2, 2, 2, 2, half, side),
        (2, 2 * side, side),
        (2, 2 * side, side),
        (2, 2, side, tile_w),
        (2 * side, side),
        (2 * side, side),
        (outer * chunk, side),
        (2 * side, side),
        (2, 2, half, side),
        (2, 2, 2, 2, rest, side),
    ]
    scratch = [
        pltpu.VMEM((4, 2 * side, 2 * side), bf16) if shape is None else pltpu.VMEM(shape, f32)
        for shape in scratch
    ]
    dma = pltpu.SemaphoreType.DMA
    scratch += [dma((8,)), dma((2, 2, 10)), dma((2, 2, 10)), dma((2, 2)), dma((2, 2)), dma((3,)), dma((3,))]
    scratch += [pltpu.SemaphoreType.REGULAR((2,))]
    smem = pl.BlockSpec(memory_space=pltpu.SMEM)
    anywhere = pl.BlockSpec(memory_space=pltpu.HBM)
    return pl.pallas_call(
        functools.partial(kernel, mesh_shape),
        out_shape=(
            jax.ShapeDtypeStruct(objects.shape, f32),
            jax.ShapeDtypeStruct(illumination.shape, f32),
        ),
        in_specs=[smem, smem] + [anywhere] * 5,
        out_specs=(pl.BlockSpec(memory_space=pl.ANY),) * 2,
        scratch_shapes=scratch,
        compiler_params=pltpu.CompilerParams(
            collective_id=0, has_side_effects=True, vmem_limit_bytes=40 * 1024 * 1024
        ),
        name="ptychography",
    )(*[in_hbm(x) for x in (row_offset, col_offset, objects, illumination, intensity, table, fresnel)])


def solution(mesh):
    table, fresnel = tables()
    shape = (mesh.shape["row"], mesh.shape["col"])

    def whole(objects, illumination, intensity, row_offset, col_offset):
        return jax.shard_map(
            functools.partial(on_device, shape),
            mesh=mesh,
            in_specs=(
                P(),
                P(),
                P(None, None, "row", "col"),
                P(),
                P(("row", "col"), None, None),
                P(("row", "col")),
                P(("row", "col")),
            ),
            out_specs=(P(None, None, "row", "col"), P()),
            check_vma=False,
        )(jnp.asarray(table), jnp.asarray(fresnel), objects, illumination, intensity, row_offset, col_offset)

    return whole
```

```python
import functools
import math

import jax
import jax.numpy as jnp
import ml_dtypes
import numpy as np
from jax import lax
from jax.experimental import pallas as pl
from jax.experimental.pallas import tpu as pltpu
from jax.sharding import PartitionSpec as P

depth = 0.5
side = 128
half = 64
tile_w = 256
count = 4
plane_rows = 8
direct = 40
rest = half - direct
plane_cols = 4
directions = ((-1, 0), (1, 0), (0, -1), (0, 1), (-1, -1), (-1, 1), (1, -1), (1, 1))
MESH = pl.DeviceIdType.MESH
f32 = jnp.float32
bf16 = jnp.bfloat16


def in_two(values):
    high = values.astype(ml_dtypes.bfloat16)
    low = (values - high.astype(np.float64)).astype(ml_dtypes.bfloat16)
    return high, low


def tables():
    index = np.arange(side)
    angle = -2.0 * math.pi / side * (index[:, None] * index[None, :] % side)
    real, imag = np.cos(angle) / math.sqrt(side), np.sin(angle) / math.sqrt(side)
    rows = np.block([[real, imag], [-imag, real]])
    cols = np.block([[real, -imag], [imag, real]])
    signed = np.where(index < side // 2, index, index - side)
    square = signed[:, None] ** 2 + signed[None, :] ** 2
    phase = -math.pi * depth / side * square
    fresnel = np.stack([np.cos(phase), np.sin(phase)]).astype(np.float32)
    return np.stack(in_two(rows) + in_two(cols)), fresnel


def split(values):
    high = values.astype(bf16)
    return high, (values - high.astype(f32)).astype(bf16)


def dot(left, right):
    return lax.dot_general(left, right, (((1,), (0,)), ((), ())), preferred_element_type=f32)


def kernel(
    mesh_shape,
    row_ref,
    col_ref,
    obj_ref,
    ill_ref,
    int_ref,
    tab_ref,
    fres_ref,
    og_ref,
    pg_ref,
    pad0,
    pad1,
    east_src,
    west_src,
    east_in,
    west_in,
    ill,
    inten,
    tab,
    fres,
    first_w,
    second_w,
    moved_s,
    acc0,
    acc1,
    fe_src,
    fw_src,
    ns_in,
    fe_in,
    fw_in,
    og,
    ar_src,
    ar_in,
    z_in,
    ar_out,
    relay_corner,
    relay_rest,
    local_sem,
    msg_send,
    msg_recv,
    relay_send,
    relay_recv,
    ar_send,
    ar_recv,
    stage_sem,
):
    n_row, n_col = mesh_shape
    row, col = lax.axis_index("row"), lax.axis_index("col")
    pads, accs = (pad0, pad1), (acc0, acc1)

    own = [
        [
            pltpu.make_async_copy(
                obj_ref.at[s, :, :, t * side : (t + 1) * side],
                pads[s].at[t + 1, :, half : half + side],
                local_sem.at[2 * s + t],
            )
            for t in range(2)
        ]
        for s in range(2)
    ]
    loads = [
        pltpu.make_async_copy(ill_ref, ill, local_sem.at[4]),
        pltpu.make_async_copy(tab_ref, tab, local_sem.at[5]),
        pltpu.make_async_copy(fres_ref, fres, local_sem.at[6]),
        pltpu.make_async_copy(int_ref, inten, local_sem.at[7]),
    ]
    for copy in own[0] + own[1] + loads:
        copy.start()

    messages = [(d, 0, half if d[1] else direct) for d in directions]
    messages += [((-1, 0), direct, rest), ((1, 0), direct, rest)]

    def halo_dst(s, m):
        (dr, dc), first, size = messages[m]
        if dc == 0:
            start = first + (3 * half if dr < 0 else 0)
            return pads[s].at[1:3, :, start : start + size]
        into = west_in if dc > 0 else east_in
        start, size = ((half, side) if dr == 0 else (3 * half, half) if dr < 0 else (0, half))
        return into.at[s, start : start + size]

    def halo_src(s, m):
        (dr, dc), first, size = messages[m]
        if dc == 0:
            start = first + (half if dr < 0 else side)
            return pads[s].at[1:3, :, start : start + size]
        start, size = ((0, side) if dr == 0 else (0, half) if dr < 0 else (half, half))
        return (east_src if dc > 0 else west_src).at[s, start : start + size]

    def fold_dst(s, m):
        (dr, dc), first, size = messages[m]
        if dc == 0:
            return ns_in.at[s, 1 if dr < 0 else 0, :, :, first : first + size]
        into = fw_in if dc > 0 else fe_in
        start, size = ((0, side) if dr == 0 else (3 * half, half) if dr < 0 else (side, half))
        return into.at[s, start : start + size]

    def fold_src(s, m):
        (dr, dc), first, size = messages[m]
        if dc == 0:
            start = first + (0 if dr < 0 else 3 * half)
            return accs[s].at[0:2, :, start : start + size]
        start, size = ((half, side) if dr == 0 else (0, half) if dr < 0 else (3 * half, half))
        return (fe_src if dc > 0 else fw_src).at[s, start : start + size]

    ends = ((halo_src, halo_dst), (fold_src, fold_dst))
    row_in, row_out = lax.rem(row, plane_rows), lax.div(row, plane_rows)
    n_out = n_row // plane_rows

    def has(dr, dc):
        found = None
        if dr:
            found = (row > 0) if dr < 0 else (row < n_row - 1)
        if dc:
            col_found = (col > 0) if dc < 0 else (col < n_col - 1)
            found = col_found if found is None else jnp.logical_and(found, col_found)
        return found

    def also(*flags):
        return functools.reduce(jnp.logical_and, [flag for flag in flags if flag is not None])

    def relayed(m):
        (dr, dc), first, _ = messages[m]
        return dr != 0 and (dc != 0 or first != 0)

    def relay_at(m):
        (dr, dc), _, _ = messages[m]
        number = 2 if dc == 0 else 1 if dc > 0 else 0
        return 2 * number + (1 if dr > 0 else 2)

    def sends(m):
        return has(*messages[m][0])

    def receives(m):
        dr, dc = messages[m][0]
        return has(-dr, -dc)

    def leaves_group(m):
        return row_in == (plane_rows - 1 if messages[m][0][0] > 0 else 0)

    def enters_group(m):
        return row_in == (0 if messages[m][0][0] > 0 else plane_rows - 1)

    def relays(m):
        dr, dc = messages[m][0]
        group = (row_out > 0) if dr < 0 else (row_out < n_out - 1)
        return also(row_in == relay_at(m), group, has(0, dc) if dc else None)

    def relay_row(m):
        dr = messages[m][0][0]
        return row + 1 - plane_rows + relay_at(m) if dr > 0 else row + relay_at(m)

    def target_of_relay(m):
        dr, dc = messages[m][0]
        return row - relay_at(m) + (plane_rows if dr > 0 else -1), col + dc

    def relay_buffer(phase, s, m):
        return (relay_rest if messages[m][0][1] == 0 else relay_corner).at[phase, s]

    def remote(src, dst, send, recv, device):
        return pltpu.make_async_remote_copy(
            src_ref=src,
            dst_ref=dst,
            send_sem=send,
            recv_sem=recv,
            device_id=device,
            device_id_type=MESH,
        )

    def straight(phase, s, m):
        src, dst = ends[phase]
        dr, dc = messages[m][0]
        return remote(
            src(s, m),
            dst(s, m),
            msg_send.at[phase, s, m],
            msg_recv.at[phase, s, m],
            (row + dr, col + dc),
        )

    def to_relay(phase, s, m):
        return remote(
            ends[phase][0](s, m),
            relay_buffer(phase, s, m),
            msg_send.at[phase, s, m],
            relay_recv.at[phase, s],
            (relay_row(m), col),
        )

    def from_relay(phase, s, m):
        return remote(
            relay_buffer(phase, s, m),
            ends[phase][1](s, m),
            relay_send.at[phase, s],
            msg_recv.at[phase, s, m],
            target_of_relay(m),
        )

    for m in range(len(messages)):

        @pl.when(jnp.logical_not(receives(m)))
        def _(m=m):
            for s in range(2):
                for dst in (halo_dst(s, m), fold_dst(s, m)):
                    dst[...] = jnp.zeros(dst.shape, f32)

    inner, outer = plane_rows * plane_cols, (n_row // plane_rows) * (n_col // plane_cols)
    outer_cols = n_col // plane_cols
    col_in, col_out = lax.rem(col, plane_cols), lax.div(col, plane_cols)
    my_inner = row_in * plane_cols + col_in
    my_outer = row_out * outer_cols + col_out

    def hops(step, size):
        return min(step, size - step)

    core_rows = plane_rows // 2
    inner_steps = [
        (y, core, x) for y in range(core_rows) for core in range(2) for x in range(plane_cols)
    ]
    inner_steps.sort(key=lambda k: -2 * (hops(k[0], core_rows) + hops(k[2], plane_cols)) - k[1])
    outer_steps = sorted(range(1, outer), key=lambda k: -hops(k, outer))

    def inner_device(step):
        y, core, x = step
        row_to = lax.rem(lax.div(row_in, 2) + y, core_rows) * 2 + lax.rem(row_in + core, 2)
        col_to = lax.rem(col_in + x, plane_cols)
        number = row_to * plane_cols + col_to
        return number, (row_out * plane_rows + row_to, col_out * plane_cols + col_to)

    def outer_device(step):
        number = lax.rem(my_outer + step, outer)
        return number, (
            lax.div(number, outer_cols) * plane_rows + row_in,
            lax.rem(number, outer_cols) * plane_cols + col_in,
        )

    barrier = pltpu.get_barrier_semaphore()
    expected = jnp.int32(0)

    def greet_if(flag, device):
        @pl.when(flag)
        def _():
            pl.semaphore_signal(barrier, inc=1, device_id=device, device_id_type=MESH)

    def greet(devices, semaphore):
        for device in devices:
            pl.semaphore_signal(semaphore, inc=1, device_id=device, device_id_type=MESH)

    def turn(index, step, size):
        return index - lax.rem(index, size) + lax.rem(lax.rem(index, size) + step, size)

    def far_row(step):
        return lax.rem(row + step * plane_rows, n_row), col

    def far_col(step):
        return row, lax.rem(col + step * plane_cols, n_col)

    line_far = [far_row(k) for k in sorted({1 % n_out, (n_out - 1) % n_out} - {0})]
    line_near = [far_col(k) for k in range(1, outer_cols)]
    line_x = [(row, turn(col, k, plane_cols)) for k in range(1, plane_cols)]
    line_y = [(turn(row, k, plane_rows), col) for k in range(1, plane_rows)]
    lines = line_far + line_near + line_y + line_x
    expected = expected + len(lines)
    greet(line_far, barrier)
    for m in range(len(messages)):
        dr, dc = messages[m][0]
        expected = expected + sends(m).astype(jnp.int32)
        if relayed(m):
            expected = expected + relays(m).astype(jnp.int32)
            greet_if(
                also(receives(m), jnp.logical_not(enters_group(m))), (row - dr, col - dc)
            )
            greet_if(
                also(receives(m), enters_group(m)),
                (row + relay_at(m) + (-plane_rows if dr > 0 else 1), col - dc),
            )
            greet_if(
                relays(m),
                (row - relay_at(m) + (plane_rows - 1 if dr > 0 else 0), col),
            )
        else:
            greet_if(receives(m), (row - dr, col - dc))
    greet(line_near + line_y + line_x, barrier)

    def second_stage():
        greet(line_far + line_x, stage_sem.at[0])

    def third_stage():
        pl.semaphore_wait(stage_sem.at[0], len(line_far + line_x))
        greet(line_near, stage_sem.at[1])

    def last_stage():
        pl.semaphore_wait(stage_sem.at[1], len(line_near))

    order = sorted(range(len(messages)), key=lambda m: not relayed(m))

    def each(phase, s, straight_do, relay_do=None):
        for m in order:
            if relayed(m):
                flag = also(sends(m), jnp.logical_not(leaves_group(m)))

                @pl.when(also(sends(m), leaves_group(m)))
                def _(m=m):
                    straight_do(to_relay(phase, s, m))

            else:
                flag = sends(m)

            @pl.when(flag)
            def _(m=m):
                straight_do(straight(phase, s, m))

            if relay_do is not None and relayed(m):

                @pl.when(relays(m))
                def _(m=m):
                    relay_do(from_relay(phase, s, m))

    def send_far(phase, s):
        for m in order:
            if messages[m][0][0]:

                @pl.when(also(sends(m), leaves_group(m)))
                def _(m=m):
                    (to_relay if relayed(m) else straight)(phase, s, m).start()

    def send_near(phase, s):
        for m in order:
            flag = sends(m)
            if messages[m][0][0]:
                flag = also(flag, jnp.logical_not(leaves_group(m)))

            @pl.when(flag)
            def _(m=m):
                straight(phase, s, m).start()

    def pass_on(phase, s):
        for m in range(len(messages)):
            if relayed(m):

                @pl.when(relays(m))
                def _(m=m):
                    to_relay(phase, s, m).wait_recv()
                    from_relay(phase, s, m).start()

    def receive_all(phase, s):
        for m in range(len(messages)):

            @pl.when(receives(m))
            def _(m=m):
                straight(phase, s, m).wait_recv()

    def sent_all(phase, s):
        each(phase, s, lambda copy: copy.wait_send(), lambda copy: copy.wait_send())

    lane = lax.broadcasted_iota(jnp.int32, (1, side), 1)
    lower = lane < half

    def pack_edges(s):
        for copy in own[s]:
            copy.wait()
        rows = slice(half, half + side)
        west_src[s] = jnp.where(
            lower, pads[s][1, 0, rows], pltpu.roll(pads[s][1, 1, rows], half, 1)
        )
        east_src[s] = jnp.where(
            lower, pltpu.roll(pads[s][2, 1, rows], half, 1), pads[s][2, 0, rows]
        )

    pack_edges(0)
    pack_edges(1)
    pl.semaphore_wait(barrier, expected)
    send_far(0, 0)
    send_far(0, 1)
    send_near(0, 0)
    second_stage()
    send_near(0, 1)

    row_at = [row_ref[j] for j in range(count)]
    col_at = [col_ref[j] for j in range(count)]
    row_grid = lax.broadcasted_iota(jnp.int32, (2 * side, side), 0)
    col_grid = lax.broadcasted_iota(jnp.int32, (2 * side, side), 1)
    place_rows = jnp.concatenate(
        [
            jnp.where(row_grid - col_grid == row_at[j], 1.0, 0.0).astype(bf16)
            for j in range(count)
        ],
        axis=1,
    )

    def lane_mask(j, k):
        offset = lane + (side * k + half) - col_at[j]
        offset = jnp.where(offset < 0, offset + 3 * side, offset)
        offset = jnp.where(offset >= 3 * side, offset - 3 * side, offset)
        return jnp.where(offset < side, 1.0, 0.0).astype(bf16)

    def join_halo(s):
        east, west = east_in[s], west_in[s]
        halo = (
            jnp.where(lower, east, west),
            pltpu.roll(jnp.where(lower, west, east), half, 1),
        )
        for part in range(2):
            pads[s][0, part] = halo[part]
            pads[s][3, part] = halo[part]

    def gather(s, out):
        for j in range(count):
            start = col_at[j] + half
            tile = lax.div(start, side)
            shift = lax.rem(start, side)
            back = lax.rem(side - shift, side)
            for part in range(2):
                near = pads[s][tile, part, pl.ds(row_at[j], side)]
                far = pads[s][tile + 1, part, pl.ds(row_at[j], side)]
                out[j * side : (j + 1) * side, part * side : (part + 1) * side] = pltpu.roll(
                    jnp.where(lane >= shift, near, far), back, 1
                )

    def by_rows(values, inverse=False):
        k = 2 if inverse else 0
        high, low = split(values)
        return dot(high, tab[k]) + dot(low, tab[k]) + dot(high, tab[k + 1])

    def by_cols(values, inverse=False):
        k = 0 if inverse else 2
        high, low = split(values)
        return dot(tab[k], high) + dot(tab[k], low) + dot(tab[k + 1], high)

    def stand(values):
        return jnp.concatenate(
            [
                jnp.concatenate(
                    [
                        values[j * side : (j + 1) * side, part * side : (part + 1) * side]
                        for j in range(count)
                    ],
                    axis=1,
                )
                for part in range(2)
            ],
            axis=0,
        )

    def lie(values):
        return jnp.concatenate(
            [
                jnp.concatenate(
                    [
                        values[part * side : (part + 1) * side, j * side : (j + 1) * side]
                        for part in range(2)
                    ],
                    axis=1,
                )
                for j in range(count)
            ],
            axis=0,
        )

    def real(values):
        return values[:, :side]

    def imag(values):
        return values[:, side:]

    def times(left, right):
        return jnp.concatenate(
            [
                real(left) * real(right) - imag(left) * imag(right),
                real(left) * imag(right) + imag(left) * real(right),
            ],
            axis=1,
        )

    def conj_times(left, right):
        return jnp.concatenate(
            [
                real(left) * real(right) + imag(left) * imag(right),
                real(left) * imag(right) - imag(left) * real(right),
            ],
            axis=1,
        )

    def propagate(values, sign):
        spectrum = by_cols(stand(by_rows(values)))
        h_real = jnp.concatenate([fres[0]] * count, axis=1)
        h_imag = jnp.concatenate([fres[1]] * count, axis=1) * sign
        s_real, s_imag = spectrum[:side], spectrum[side:]
        spectrum = jnp.concatenate(
            [s_real * h_real - s_imag * h_imag, s_real * h_imag + s_imag * h_real], axis=0
        )
        return by_rows(lie(by_cols(spectrum, True)), True)

    def place(s, values):
        pieces = ([], [])
        for j in range(count):
            start = lax.rem(col_at[j] + half, side)
            masks = [lane_mask(j, k) for k in range(3)]
            for part in range(2):
                window = values[j * side : (j + 1) * side, part * side : (part + 1) * side]
                for piece, block in zip(pieces, split(pltpu.roll(window, start, 1))):
                    piece.append(jnp.concatenate([block * m for m in masks], axis=1))
        total = None
        for piece in pieces:
            both = jnp.concatenate(
                [
                    jnp.concatenate([piece[2 * j], piece[2 * j + 1]], axis=1)
                    for j in range(count)
                ],
                axis=0,
            )
            part_sum = dot(place_rows, both)
            total = part_sum if total is None else total + part_sum
        for part in range(2):
            for tile in range(3):
                start = (3 * part + tile) * side
                accs[s][tile, part] = total[:, start : start + side]
        halo_real, halo_imag = total[:, 2 * side : 3 * side], total[:, 5 * side :]
        turned = pltpu.roll(halo_imag, half, 1)
        fe_src[s] = jnp.where(lower, halo_real, turned)
        fw_src[s] = jnp.where(lower, turned, halo_real)

    def finish(s):
        from_west = fw_in[s, 0:side] + fw_in[s, side : 2 * side]
        from_east = fe_in[s, 0:side] + fe_in[s, side : 2 * side]
        for part in range(2):
            if part:
                from_west = pltpu.roll(from_west, half, 1)
                from_east = pltpu.roll(from_east, half, 1)
            rows = slice(half, half + side)
            for tile in range(2):
                beside = jnp.where(lower == (tile == 0), from_east if tile else from_west, 0.0)
                above_below = jnp.concatenate(
                    [ns_in[s, 0, tile, part], ns_in[s, 1, tile, part]], axis=0
                )
                og[s, part, :, tile * side : (tile + 1) * side] = (
                    accs[s][tile, part, rows] + above_below + beside
                )
        out_copy(s).start()

    def out_copy(s):
        return pltpu.make_async_copy(og.at[s], og_ref.at[s], local_sem.at[s])

    for copy in loads[:3]:
        copy.wait()
    illumination = jnp.concatenate([ill[0], ill[1]], axis=1)
    probe = jnp.concatenate([illumination] * count, axis=0)

    pass_on(0, 0)
    receive_all(0, 0)
    join_halo(0)
    gather(0, first_w)
    pass_on(0, 1)
    third_stage()
    moved_s[...] = propagate(times(probe, first_w[...]), 1.0)

    receive_all(0, 1)
    join_halo(1)
    gather(1, second_w)
    far = by_cols(stand(by_rows(times(moved_s[...], second_w[...]))))
    loads[3].wait()
    measured = jnp.concatenate([inten[j] for j in range(count)], axis=1)
    far_real, far_imag = far[:side], far[side:]
    residual = far_real * far_real + far_imag * far_imag - measured
    far_grad = jnp.concatenate([far_real * residual, far_imag * residual], axis=0)
    exit_grad = by_rows(lie(by_cols(far_grad, True)), True)


    entry_grad = propagate(conj_times(second_w[...], exit_grad), -1.0)
    probe_local = conj_times(first_w[...], entry_grad)
    probe_local = sum(probe_local[j * side : (j + 1) * side] for j in range(count))
    ar_src[0:side] = real(probe_local)
    ar_src[side : 2 * side] = imag(probe_local)

    chunk = 2 * side // inner

    def rows_of(number):
        return pl.ds(pl.multiple_of(number * chunk, chunk), chunk)

    def scatter_copy(k):
        number, device = inner_device(k)
        return pltpu.make_async_remote_copy(
            src_ref=ar_src.at[rows_of(number)],
            dst_ref=ar_in.at[rows_of(my_inner)],
            send_sem=ar_send.at[0],
            recv_sem=ar_recv.at[0],
            device_id=device,
            device_id_type=MESH,
        )

    def outer_copy(k):
        number, device = outer_device(k)
        return pltpu.make_async_remote_copy(
            src_ref=z_in.at[rows_of(my_outer)],
            dst_ref=z_in.at[rows_of(my_outer)],
            send_sem=ar_send.at[1],
            recv_sem=ar_recv.at[1],
            device_id=device,
            device_id_type=MESH,
        )

    def gather_copy(k):
        number, device = inner_device(k)
        return pltpu.make_async_remote_copy(
            src_ref=ar_out.at[rows_of(my_inner)],
            dst_ref=ar_out.at[rows_of(my_inner)],
            send_sem=ar_send.at[2],
            recv_sem=ar_recv.at[2],
            device_id=device,
            device_id_type=MESH,
        )

    def start_many(copy_of, steps):
        for step in steps:
            copy_of(step).start()

    def wait_many(buffer, number, sem):
        if number == 1:
            return
        part = buffer.at[0 : (number - 1) * chunk]
        pltpu.make_async_copy(part, part, sem).wait()

    start_many(scatter_copy, inner_steps[:-1])
    place(1, conj_times(moved_s[...], exit_grad))
    place(0, conj_times(probe, entry_grad))

    ar_in[rows_of(my_inner)] = ar_src[rows_of(my_inner)]
    wait_many(ar_in, inner, ar_recv.at[0])
    z_in[rows_of(my_outer)] = sum(ar_in[k * chunk : (k + 1) * chunk] for k in range(inner))
    last_stage()
    start_many(outer_copy, outer_steps)
    send_far(1, 1)
    send_far(1, 0)
    send_near(1, 1)
    send_near(1, 0)
    pass_on(1, 1)
    pass_on(1, 0)


    wait_many(z_in, outer, ar_recv.at[1])
    positions = count * n_row * n_col
    ar_out[rows_of(my_inner)] = sum(z_in[k * chunk : (k + 1) * chunk] for k in range(outer)) * (
        1.0 / math.sqrt(positions)
    )
    start_many(gather_copy, inner_steps[:-1])

    receive_all(1, 1)
    finish(1)
    receive_all(1, 0)
    finish(0)

    wait_many(ar_src, inner, ar_send.at[0])
    wait_many(z_in, outer, ar_send.at[1])
    for s in range(2):
        sent_all(0, s)
        sent_all(1, s)
    wait_many(ar_out, inner, ar_recv.at[2])
    probe_copies = [
        pltpu.make_async_copy(
            ar_out.at[part * side : (part + 1) * side], pg_ref.at[part], local_sem.at[2 + part]
        )
        for part in range(2)
    ]
    for copy in probe_copies:
        copy.start()
    wait_many(ar_out, inner, ar_send.at[2])
    for s in range(2):
        out_copy(s).wait()
    for copy in probe_copies:
        copy.wait()


def in_hbm(x):
    return pltpu.with_memory_space_constraint(x, pltpu.HBM)


def on_device(mesh_shape, table, fresnel, objects, illumination, intensity, row_offset, col_offset):
    n_row, n_col = mesh_shape
    outer = (n_row // plane_rows) * (n_col // plane_cols)
    chunk = 2 * side // (plane_rows * plane_cols)
    scratch = [
        (4, 2, 2 * side, side),
        (4, 2, 2 * side, side),
        (2, side, side),
        (2, side, side),
        (2, 2 * side, side),
        (2, 2 * side, side),
        (2, side, side),
        (count, side, side),
        None,
        (2, side, side),
        (count * side, 2 * side),
        (count * side, 2 * side),
        (count * side, 2 * side),
        (3, 2, 2 * side, side),
        (3, 2, 2 * side, side),
        (2, 2 * side, side),
        (2, 2 * side, side),
        (2, 2, 2, 2, half, side),
        (2, 2 * side, side),
        (2, 2 * side, side),
        (2, 2, side, tile_w),
        (2 * side, side),
        (2 * side, side),
        (outer * chunk, side),
        (2 * side, side),
        (2, 2, half, side),
        (2, 2, 2, 2, rest, side),
    ]
    scratch = [
        pltpu.VMEM((4, 2 * side, 2 * side), bf16) if shape is None else pltpu.VMEM(shape, f32)
        for shape in scratch
    ]
    dma = pltpu.SemaphoreType.DMA
    scratch += [dma((8,)), dma((2, 2, 10)), dma((2, 2, 10)), dma((2, 2)), dma((2, 2)), dma((3,)), dma((3,))]
    scratch += [pltpu.SemaphoreType.REGULAR((2,))]
    smem = pl.BlockSpec(memory_space=pltpu.SMEM)
    anywhere = pl.BlockSpec(memory_space=pltpu.HBM)
    return pl.pallas_call(
        functools.partial(kernel, mesh_shape),
        out_shape=(
            jax.ShapeDtypeStruct(objects.shape, f32),
            jax.ShapeDtypeStruct(illumination.shape, f32),
        ),
        in_specs=[smem, smem] + [anywhere] * 5,
        out_specs=(pl.BlockSpec(memory_space=pl.ANY),) * 2,
        scratch_shapes=scratch,
        compiler_params=pltpu.CompilerParams(
            collective_id=0, has_side_effects=True, vmem_limit_bytes=40 * 1024 * 1024
        ),
        name="ptychography",
    )(*[in_hbm(x) for x in (row_offset, col_offset, objects, illumination, intensity, table, fresnel)])


def solution(mesh):
    table, fresnel = tables()
    shape = (mesh.shape["row"], mesh.shape["col"])

    def whole(objects, illumination, intensity, row_offset, col_offset):
        return jax.shard_map(
            functools.partial(on_device, shape),
            mesh=mesh,
            in_specs=(
                P(),
                P(),
                P(None, None, "row", "col"),
                P(),
                P(("row", "col"), None, None),
                P(("row", "col")),
                P(("row", "col")),
            ),
            out_specs=(P(None, None, "row", "col"), P()),
            check_vma=False,
        )(jnp.asarray(table), jnp.asarray(fresnel), objects, illumination, intensity, row_offset, col_offset)

    return whole
```

```python
import functools
import math

import jax
import jax.numpy as jnp
import ml_dtypes
import numpy as np
from jax import lax
from jax.experimental import pallas as pl
from jax.experimental.pallas import tpu as pltpu
from jax.sharding import PartitionSpec as P

depth = 0.5
side = 128
half = 64
tile_w = 256
count = 4
plane_rows = 8
direct = 40
rest = half - direct
plane_cols = 4
directions = ((-1, 0), (1, 0), (0, -1), (0, 1), (-1, -1), (-1, 1), (1, -1), (1, 1))
MESH = pl.DeviceIdType.MESH
f32 = jnp.float32
bf16 = jnp.bfloat16


def in_two(values):
    high = values.astype(ml_dtypes.bfloat16)
    low = (values - high.astype(np.float64)).astype(ml_dtypes.bfloat16)
    return high, low


def tables():
    index = np.arange(side)
    angle = -2.0 * math.pi / side * (index[:, None] * index[None, :] % side)
    real, imag = np.cos(angle) / math.sqrt(side), np.sin(angle) / math.sqrt(side)
    rows = np.block([[real, imag], [-imag, real]])
    cols = np.block([[real, -imag], [imag, real]])
    signed = np.where(index < side // 2, index, index - side)
    square = signed[:, None] ** 2 + signed[None, :] ** 2
    phase = -math.pi * depth / side * square
    fresnel = np.stack([np.cos(phase), np.sin(phase)]).astype(np.float32)
    return np.stack(in_two(rows) + in_two(cols)), fresnel


def split(values):
    high = values.astype(bf16)
    return high, (values - high.astype(f32)).astype(bf16)


def dot(left, right):
    return lax.dot_general(left, right, (((1,), (0,)), ((), ())), preferred_element_type=f32)


def kernel(
    mesh_shape,
    row_ref,
    col_ref,
    obj_ref,
    ill_ref,
    int_ref,
    tab_ref,
    fres_ref,
    og_ref,
    pg_ref,
    pad0,
    pad1,
    east_src,
    west_src,
    east_in,
    west_in,
    ill,
    inten,
    tab,
    fres,
    first_w,
    second_w,
    moved_s,
    acc0,
    acc1,
    fe_src,
    fw_src,
    ns_in,
    fe_in,
    fw_in,
    og,
    ar_src,
    ar_in,
    z_in,
    ar_out,
    relay_corner,
    relay_rest,
    local_sem,
    msg_send,
    msg_recv,
    relay_send,
    relay_recv,
    ar_send,
    ar_recv,
    stage_sem,
):
    n_row, n_col = mesh_shape
    row, col = lax.axis_index("row"), lax.axis_index("col")
    pads, accs = (pad0, pad1), (acc0, acc1)

    own = [
        [
            pltpu.make_async_copy(
                obj_ref.at[s, :, :, t * side : (t + 1) * side],
                pads[s].at[t + 1, :, half : half + side],
                local_sem.at[2 * s + t],
            )
            for t in range(2)
        ]
        for s in range(2)
    ]
    loads = [
        pltpu.make_async_copy(ill_ref, ill, local_sem.at[4]),
        pltpu.make_async_copy(tab_ref, tab, local_sem.at[5]),
        pltpu.make_async_copy(fres_ref, fres, local_sem.at[6]),
        pltpu.make_async_copy(int_ref, inten, local_sem.at[7]),
    ]
    for copy in own[0] + own[1] + loads:
        copy.start()

    messages = [(d, 0, half if d[1] else direct) for d in directions]
    messages += [((-1, 0), direct, rest), ((1, 0), direct, rest)]

    def halo_dst(s, m):
        (dr, dc), first, size = messages[m]
        if dc == 0:
            start = first + (3 * half if dr < 0 else 0)
            return pads[s].at[1:3, :, start : start + size]
        into = west_in if dc > 0 else east_in
        start, size = ((half, side) if dr == 0 else (3 * half, half) if dr < 0 else (0, half))
        return into.at[s, start : start + size]

    def halo_src(s, m):
        (dr, dc), first, size = messages[m]
        if dc == 0:
            start = first + (half if dr < 0 else side)
            return pads[s].at[1:3, :, start : start + size]
        start, size = ((0, side) if dr == 0 else (0, half) if dr < 0 else (half, half))
        return (east_src if dc > 0 else west_src).at[s, start : start + size]

    def fold_dst(s, m):
        (dr, dc), first, size = messages[m]
        if dc == 0:
            return ns_in.at[s, 1 if dr < 0 else 0, :, :, first : first + size]
        into = fw_in if dc > 0 else fe_in
        start, size = ((0, side) if dr == 0 else (3 * half, half) if dr < 0 else (side, half))
        return into.at[s, start : start + size]

    def fold_src(s, m):
        (dr, dc), first, size = messages[m]
        if dc == 0:
            start = first + (0 if dr < 0 else 3 * half)
            return accs[s].at[0:2, :, start : start + size]
        start, size = ((half, side) if dr == 0 else (0, half) if dr < 0 else (3 * half, half))
        return (fe_src if dc > 0 else fw_src).at[s, start : start + size]

    ends = ((halo_src, halo_dst), (fold_src, fold_dst))
    row_in, row_out = lax.rem(row, plane_rows), lax.div(row, plane_rows)
    n_out = n_row // plane_rows

    def has(dr, dc):
        found = None
        if dr:
            found = (row > 0) if dr < 0 else (row < n_row - 1)
        if dc:
            col_found = (col > 0) if dc < 0 else (col < n_col - 1)
            found = col_found if found is None else jnp.logical_and(found, col_found)
        return found

    def also(*flags):
        return functools.reduce(jnp.logical_and, [flag for flag in flags if flag is not None])

    def relayed(m):
        (dr, dc), first, _ = messages[m]
        return dr != 0 and (dc != 0 or first != 0)

    def relay_at(m):
        (dr, dc), _, _ = messages[m]
        number = 2 if dc == 0 else 1 if dc > 0 else 0
        return 2 * number + (1 if dr > 0 else 2)

    def sends(m):
        return has(*messages[m][0])

    def receives(m):
        dr, dc = messages[m][0]
        return has(-dr, -dc)

    def leaves_group(m):
        return row_in == (plane_rows - 1 if messages[m][0][0] > 0 else 0)

    def enters_group(m):
        return row_in == (0 if messages[m][0][0] > 0 else plane_rows - 1)

    def relays(m):
        dr, dc = messages[m][0]
        group = (row_out > 0) if dr < 0 else (row_out < n_out - 1)
        return also(row_in == relay_at(m), group, has(0, dc) if dc else None)

    def relay_row(m):
        dr = messages[m][0][0]
        return row + 1 - plane_rows + relay_at(m) if dr > 0 else row + relay_at(m)

    def target_of_relay(m):
        dr, dc = messages[m][0]
        return row - relay_at(m) + (plane_rows if dr > 0 else -1), col + dc

    def relay_buffer(phase, s, m):
        return (relay_rest if messages[m][0][1] == 0 else relay_corner).at[phase, s]

    def remote(src, dst, send, recv, device):
        return pltpu.make_async_remote_copy(
            src_ref=src,
            dst_ref=dst,
            send_sem=send,
            recv_sem=recv,
            device_id=device,
            device_id_type=MESH,
        )

    def straight(phase, s, m):
        src, dst = ends[phase]
        dr, dc = messages[m][0]
        return remote(
            src(s, m),
            dst(s, m),
            msg_send.at[phase, s, m],
            msg_recv.at[phase, s, m],
            (row + dr, col + dc),
        )

    def to_relay(phase, s, m):
        return remote(
            ends[phase][0](s, m),
            relay_buffer(phase, s, m),
            msg_send.at[phase, s, m],
            relay_recv.at[phase, s],
            (relay_row(m), col),
        )

    def from_relay(phase, s, m):
        return remote(
            relay_buffer(phase, s, m),
            ends[phase][1](s, m),
            relay_send.at[phase, s],
            msg_recv.at[phase, s, m],
            target_of_relay(m),
        )

    for m in range(len(messages)):

        @pl.when(jnp.logical_not(receives(m)))
        def _(m=m):
            for s in range(2):
                for dst in (halo_dst(s, m), fold_dst(s, m)):
                    dst[...] = jnp.zeros(dst.shape, f32)

    inner, outer = plane_rows * plane_cols, (n_row // plane_rows) * (n_col // plane_cols)
    outer_cols = n_col // plane_cols
    col_in, col_out = lax.rem(col, plane_cols), lax.div(col, plane_cols)
    my_inner = row_in * plane_cols + col_in
    my_outer = row_out * outer_cols + col_out

    def hops(step, size):
        return min(step, size - step)

    core_rows = plane_rows // 2
    inner_steps = [
        (y, core, x) for y in range(core_rows) for core in range(2) for x in range(plane_cols)
    ]
    inner_steps.sort(key=lambda k: -2 * (hops(k[0], core_rows) + hops(k[2], plane_cols)) - k[1])
    outer_steps = sorted(range(1, outer), key=lambda k: -hops(k, outer))

    def inner_device(step):
        y, core, x = step
        row_to = lax.rem(lax.div(row_in, 2) + y, core_rows) * 2 + lax.rem(row_in + core, 2)
        col_to = lax.rem(col_in + x, plane_cols)
        number = row_to * plane_cols + col_to
        return number, (row_out * plane_rows + row_to, col_out * plane_cols + col_to)

    def outer_device(step):
        number = lax.rem(my_outer + step, outer)
        return number, (
            lax.div(number, outer_cols) * plane_rows + row_in,
            lax.rem(number, outer_cols) * plane_cols + col_in,
        )

    barrier = pltpu.get_barrier_semaphore()
    expected = jnp.int32(0)

    def greet_if(flag, device):
        @pl.when(flag)
        def _():
            pl.semaphore_signal(barrier, inc=1, device_id=device, device_id_type=MESH)

    def greet(devices, semaphore):
        for device in devices:
            pl.semaphore_signal(semaphore, inc=1, device_id=device, device_id_type=MESH)

    def turn(index, step, size):
        return index - lax.rem(index, size) + lax.rem(lax.rem(index, size) + step, size)

    def far_row(step):
        return lax.rem(row + step * plane_rows, n_row), col

    def far_col(step):
        return row, lax.rem(col + step * plane_cols, n_col)

    line_far = [far_row(k) for k in sorted({1 % n_out, (n_out - 1) % n_out} - {0})]
    line_near = [far_col(k) for k in range(1, outer_cols)]
    line_x = [(row, turn(col, k, plane_cols)) for k in range(1, plane_cols)]
    line_y = [(turn(row, k, plane_rows), col) for k in range(1, plane_rows)]
    lines = line_far + line_near + line_y + line_x
    expected = expected + len(lines)
    greet(line_far, barrier)
    for m in range(len(messages)):
        dr, dc = messages[m][0]
        expected = expected + sends(m).astype(jnp.int32)
        if relayed(m):
            expected = expected + relays(m).astype(jnp.int32)
            greet_if(
                also(receives(m), jnp.logical_not(enters_group(m))), (row - dr, col - dc)
            )
            greet_if(
                also(receives(m), enters_group(m)),
                (row + relay_at(m) + (-plane_rows if dr > 0 else 1), col - dc),
            )
            greet_if(
                relays(m),
                (row - relay_at(m) + (plane_rows - 1 if dr > 0 else 0), col),
            )
        else:
            greet_if(receives(m), (row - dr, col - dc))
    greet(line_near + line_y + line_x, barrier)

    def second_stage():
        greet(line_far + line_x, stage_sem.at[0])

    def third_stage():
        pl.semaphore_wait(stage_sem.at[0], len(line_far + line_x))
        greet(line_near, stage_sem.at[1])

    def last_stage():
        pl.semaphore_wait(stage_sem.at[1], len(line_near))

    order = sorted(range(len(messages)), key=lambda m: not relayed(m))

    def each(phase, s, straight_do, relay_do=None):
        for m in order:
            if relayed(m):
                flag = also(sends(m), jnp.logical_not(leaves_group(m)))

                @pl.when(also(sends(m), leaves_group(m)))
                def _(m=m):
                    straight_do(to_relay(phase, s, m))

            else:
                flag = sends(m)

            @pl.when(flag)
            def _(m=m):
                straight_do(straight(phase, s, m))

            if relay_do is not None and relayed(m):

                @pl.when(relays(m))
                def _(m=m):
                    relay_do(from_relay(phase, s, m))

    def send_far(phase, s):
        for m in order:
            if messages[m][0][0]:

                @pl.when(also(sends(m), leaves_group(m)))
                def _(m=m):
                    (to_relay if relayed(m) else straight)(phase, s, m).start()

    def send_near(phase, s):
        for m in order:
            flag = sends(m)
            if messages[m][0][0]:
                flag = also(flag, jnp.logical_not(leaves_group(m)))

            @pl.when(flag)
            def _(m=m):
                straight(phase, s, m).start()

    def pass_on(phase, s):
        for m in range(len(messages)):
            if relayed(m):

                @pl.when(relays(m))
                def _(m=m):
                    to_relay(phase, s, m).wait_recv()
                    from_relay(phase, s, m).start()

    def receive_all(phase, s):
        for m in range(len(messages)):

            @pl.when(receives(m))
            def _(m=m):
                straight(phase, s, m).wait_recv()

    def sent_all(phase, s):
        each(phase, s, lambda copy: copy.wait_send(), lambda copy: copy.wait_send())

    lane = lax.broadcasted_iota(jnp.int32, (1, side), 1)
    lower = lane < half

    def pack_edges(s):
        for copy in own[s]:
            copy.wait()
        rows = slice(half, half + side)
        west_src[s] = jnp.where(
            lower, pads[s][1, 0, rows], pltpu.roll(pads[s][1, 1, rows], half, 1)
        )
        east_src[s] = jnp.where(
            lower, pltpu.roll(pads[s][2, 1, rows], half, 1), pads[s][2, 0, rows]
        )

    pack_edges(0)
    pack_edges(1)
    pl.semaphore_wait(barrier, expected)
    send_far(0, 0)
    send_far(0, 1)
    send_near(0, 0)
    second_stage()
    send_near(0, 1)

    row_at = [row_ref[j] for j in range(count)]
    col_at = [col_ref[j] for j in range(count)]
    row_grid = lax.broadcasted_iota(jnp.int32, (2 * side, side), 0)
    col_grid = lax.broadcasted_iota(jnp.int32, (2 * side, side), 1)
    place_rows = jnp.concatenate(
        [
            jnp.where(row_grid - col_grid == row_at[j], 1.0, 0.0).astype(bf16)
            for j in range(count)
        ],
        axis=1,
    )

    def lane_mask(j, k):
        offset = lane + (side * k + half) - col_at[j]
        offset = jnp.where(offset < 0, offset + 3 * side, offset)
        offset = jnp.where(offset >= 3 * side, offset - 3 * side, offset)
        return jnp.where(offset < side, 1.0, 0.0).astype(bf16)

    def join_halo(s):
        east, west = east_in[s], west_in[s]
        halo = (
            jnp.where(lower, east, west),
            pltpu.roll(jnp.where(lower, west, east), half, 1),
        )
        for part in range(2):
            pads[s][0, part] = halo[part]
            pads[s][3, part] = halo[part]

    def gather(s, out):
        for j in range(count):
            start = col_at[j] + half
            tile = lax.div(start, side)
            shift = lax.rem(start, side)
            back = lax.rem(side - shift, side)
            for part in range(2):
                near = pads[s][tile, part, pl.ds(row_at[j], side)]
                far = pads[s][tile + 1, part, pl.ds(row_at[j], side)]
                out[j * side : (j + 1) * side, part * side : (part + 1) * side] = pltpu.roll(
                    jnp.where(lane >= shift, near, far), back, 1
                )

    def by_rows(values, inverse=False):
        k = 2 if inverse else 0
        high, low = split(values)
        return dot(high, tab[k]) + dot(low, tab[k]) + dot(high, tab[k + 1])

    def by_cols(values, inverse=False):
        k = 0 if inverse else 2
        high, low = split(values)
        return dot(tab[k], high) + dot(tab[k], low) + dot(tab[k + 1], high)

    def stand(values):
        return jnp.concatenate(
            [
                jnp.concatenate(
                    [
                        values[j * side : (j + 1) * side, part * side : (part + 1) * side]
                        for j in range(count)
                    ],
                    axis=1,
                )
                for part in range(2)
            ],
            axis=0,
        )

    def lie(values):
        return jnp.concatenate(
            [
                jnp.concatenate(
                    [
                        values[part * side : (part + 1) * side, j * side : (j + 1) * side]
                        for part in range(2)
                    ],
                    axis=1,
                )
                for j in range(count)
            ],
            axis=0,
        )

    def real(values):
        return values[:, :side]

    def imag(values):
        return values[:, side:]

    def times(left, right):
        return jnp.concatenate(
            [
                real(left) * real(right) - imag(left) * imag(right),
                real(left) * imag(right) + imag(left) * real(right),
            ],
            axis=1,
        )

    def conj_times(left, right):
        return jnp.concatenate(
            [
                real(left) * real(right) + imag(left) * imag(right),
                real(left) * imag(right) - imag(left) * real(right),
            ],
            axis=1,
        )

    def propagate(values, sign):
        spectrum = by_cols(stand(by_rows(values)))
        h_real = jnp.concatenate([fres[0]] * count, axis=1)
        h_imag = jnp.concatenate([fres[1]] * count, axis=1) * sign
        s_real, s_imag = spectrum[:side], spectrum[side:]
        spectrum = jnp.concatenate(
            [s_real * h_real - s_imag * h_imag, s_real * h_imag + s_imag * h_real], axis=0
        )
        return by_rows(lie(by_cols(spectrum, True)), True)

    def place(s, values):
        pieces = ([], [])
        for j in range(count):
            start = lax.rem(col_at[j] + half, side)
            masks = [lane_mask(j, k) for k in range(3)]
            for part in range(2):
                window = values[j * side : (j + 1) * side, part * side : (part + 1) * side]
                for piece, block in zip(pieces, split(pltpu.roll(window, start, 1))):
                    piece.append(jnp.concatenate([block * m for m in masks], axis=1))
        total = None
        for piece in pieces:
            both = jnp.concatenate(
                [
                    jnp.concatenate([piece[2 * j], piece[2 * j + 1]], axis=1)
                    for j in range(count)
                ],
                axis=0,
            )
            part_sum = dot(place_rows, both)
            total = part_sum if total is None else total + part_sum
        for part in range(2):
            for tile in range(3):
                start = (3 * part + tile) * side
                accs[s][tile, part] = total[:, start : start + side]
        halo_real, halo_imag = total[:, 2 * side : 3 * side], total[:, 5 * side :]
        turned = pltpu.roll(halo_imag, half, 1)
        fe_src[s] = jnp.where(lower, halo_real, turned)
        fw_src[s] = jnp.where(lower, turned, halo_real)

    def finish(s):
        from_west = fw_in[s, 0:side] + fw_in[s, side : 2 * side]
        from_east = fe_in[s, 0:side] + fe_in[s, side : 2 * side]
        for part in range(2):
            if part:
                from_west = pltpu.roll(from_west, half, 1)
                from_east = pltpu.roll(from_east, half, 1)
            rows = slice(half, half + side)
            for tile in range(2):
                beside = jnp.where(lower == (tile == 0), from_east if tile else from_west, 0.0)
                above_below = jnp.concatenate(
                    [ns_in[s, 0, tile, part], ns_in[s, 1, tile, part]], axis=0
                )
                og[s, part, :, tile * side : (tile + 1) * side] = (
                    accs[s][tile, part, rows] + above_below + beside
                )
        out_copy(s).start()

    def out_copy(s):
        return pltpu.make_async_copy(og.at[s], og_ref.at[s], local_sem.at[s])

    for copy in loads[:3]:
        copy.wait()
    illumination = jnp.concatenate([ill[0], ill[1]], axis=1)
    probe = jnp.concatenate([illumination] * count, axis=0)

    pass_on(0, 0)
    pass_on(0, 1)
    receive_all(0, 0)
    join_halo(0)
    gather(0, first_w)
    third_stage()
    moved_s[...] = propagate(times(probe, first_w[...]), 1.0)

    receive_all(0, 1)
    join_halo(1)
    gather(1, second_w)
    far = by_cols(stand(by_rows(times(moved_s[...], second_w[...]))))
    loads[3].wait()
    measured = jnp.concatenate([inten[j] for j in range(count)], axis=1)
    far_real, far_imag = far[:side], far[side:]
    residual = far_real * far_real + far_imag * far_imag - measured
    far_grad = jnp.concatenate([far_real * residual, far_imag * residual], axis=0)
    exit_grad = by_rows(lie(by_cols(far_grad, True)), True)


    entry_grad = propagate(conj_times(second_w[...], exit_grad), -1.0)
    probe_local = conj_times(first_w[...], entry_grad)
    probe_local = sum(probe_local[j * side : (j + 1) * side] for j in range(count))
    ar_src[0:side] = real(probe_local)
    ar_src[side : 2 * side] = imag(probe_local)

    chunk = 2 * side // inner

    def rows_of(number):
        return pl.ds(pl.multiple_of(number * chunk, chunk), chunk)

    def scatter_copy(k):
        number, device = inner_device(k)
        return pltpu.make_async_remote_copy(
            src_ref=ar_src.at[rows_of(number)],
            dst_ref=ar_in.at[rows_of(my_inner)],
            send_sem=ar_send.at[0],
            recv_sem=ar_recv.at[0],
            device_id=device,
            device_id_type=MESH,
        )

    def outer_copy(k):
        number, device = outer_device(k)
        return pltpu.make_async_remote_copy(
            src_ref=z_in.at[rows_of(my_outer)],
            dst_ref=z_in.at[rows_of(my_outer)],
            send_sem=ar_send.at[1],
            recv_sem=ar_recv.at[1],
            device_id=device,
            device_id_type=MESH,
        )

    def gather_copy(k):
        number, device = inner_device(k)
        return pltpu.make_async_remote_copy(
            src_ref=ar_out.at[rows_of(my_inner)],
            dst_ref=ar_out.at[rows_of(my_inner)],
            send_sem=ar_send.at[2],
            recv_sem=ar_recv.at[2],
            device_id=device,
            device_id_type=MESH,
        )

    def start_many(copy_of, steps):
        for step in steps:
            copy_of(step).start()

    def wait_many(buffer, number, sem):
        if number == 1:
            return
        part = buffer.at[0 : (number - 1) * chunk]
        pltpu.make_async_copy(part, part, sem).wait()

    start_many(scatter_copy, inner_steps[:-1])
    place(1, conj_times(moved_s[...], exit_grad))
    place(0, conj_times(probe, entry_grad))

    ar_in[rows_of(my_inner)] = ar_src[rows_of(my_inner)]
    last_stage()
    wait_many(ar_in, inner, ar_recv.at[0])
    z_in[rows_of(my_outer)] = sum(ar_in[k * chunk : (k + 1) * chunk] for k in range(inner))
    start_many(outer_copy, outer_steps)
    send_far(1, 1)
    send_far(1, 0)
    send_near(1, 1)
    send_near(1, 0)
    pass_on(1, 1)
    pass_on(1, 0)


    wait_many(z_in, outer, ar_recv.at[1])
    positions = count * n_row * n_col
    ar_out[rows_of(my_inner)] = sum(z_in[k * chunk : (k + 1) * chunk] for k in range(outer)) * (
        1.0 / math.sqrt(positions)
    )
    start_many(gather_copy, inner_steps[:-1])

    receive_all(1, 1)
    finish(1)
    receive_all(1, 0)
    finish(0)

    wait_many(ar_src, inner, ar_send.at[0])
    wait_many(z_in, outer, ar_send.at[1])
    for s in range(2):
        sent_all(0, s)
        sent_all(1, s)
    wait_many(ar_out, inner, ar_recv.at[2])
    probe_copies = [
        pltpu.make_async_copy(
            ar_out.at[part * side : (part + 1) * side], pg_ref.at[part], local_sem.at[2 + part]
        )
        for part in range(2)
    ]
    for copy in probe_copies:
        copy.start()
    wait_many(ar_out, inner, ar_send.at[2])
    for s in range(2):
        out_copy(s).wait()
    for copy in probe_copies:
        copy.wait()


def in_hbm(x):
    return pltpu.with_memory_space_constraint(x, pltpu.HBM)


def on_device(mesh_shape, table, fresnel, objects, illumination, intensity, row_offset, col_offset):
    n_row, n_col = mesh_shape
    outer = (n_row // plane_rows) * (n_col // plane_cols)
    chunk = 2 * side // (plane_rows * plane_cols)
    scratch = [
        (4, 2, 2 * side, side),
        (4, 2, 2 * side, side),
        (2, side, side),
        (2, side, side),
        (2, 2 * side, side),
        (2, 2 * side, side),
        (2, side, side),
        (count, side, side),
        None,
        (2, side, side),
        (count * side, 2 * side),
        (count * side, 2 * side),
        (count * side, 2 * side),
        (3, 2, 2 * side, side),
        (3, 2, 2 * side, side),
        (2, 2 * side, side),
        (2, 2 * side, side),
        (2, 2, 2, 2, half, side),
        (2, 2 * side, side),
        (2, 2 * side, side),
        (2, 2, side, tile_w),
        (2 * side, side),
        (2 * side, side),
        (outer * chunk, side),
        (2 * side, side),
        (2, 2, half, side),
        (2, 2, 2, 2, rest, side),
    ]
    scratch = [
        pltpu.VMEM((4, 2 * side, 2 * side), bf16) if shape is None else pltpu.VMEM(shape, f32)
        for shape in scratch
    ]
    dma = pltpu.SemaphoreType.DMA
    scratch += [dma((8,)), dma((2, 2, 10)), dma((2, 2, 10)), dma((2, 2)), dma((2, 2)), dma((3,)), dma((3,))]
    scratch += [pltpu.SemaphoreType.REGULAR((2,))]
    smem = pl.BlockSpec(memory_space=pltpu.SMEM)
    anywhere = pl.BlockSpec(memory_space=pltpu.HBM)
    return pl.pallas_call(
        functools.partial(kernel, mesh_shape),
        out_shape=(
            jax.ShapeDtypeStruct(objects.shape, f32),
            jax.ShapeDtypeStruct(illumination.shape, f32),
        ),
        in_specs=[smem, smem] + [anywhere] * 5,
        out_specs=(pl.BlockSpec(memory_space=pl.ANY),) * 2,
        scratch_shapes=scratch,
        compiler_params=pltpu.CompilerParams(
            collective_id=0, has_side_effects=True, vmem_limit_bytes=40 * 1024 * 1024
        ),
        name="ptychography",
    )(*[in_hbm(x) for x in (row_offset, col_offset, objects, illumination, intensity, table, fresnel)])


def solution(mesh):
    table, fresnel = tables()
    shape = (mesh.shape["row"], mesh.shape["col"])

    def whole(objects, illumination, intensity, row_offset, col_offset):
        return jax.shard_map(
            functools.partial(on_device, shape),
            mesh=mesh,
            in_specs=(
                P(),
                P(),
                P(None, None, "row", "col"),
                P(),
                P(("row", "col"), None, None),
                P(("row", "col")),
                P(("row", "col")),
            ),
            out_specs=(P(None, None, "row", "col"), P()),
            check_vma=False,
        )(jnp.asarray(table), jnp.asarray(fresnel), objects, illumination, intensity, row_offset, col_offset)

    return whole
```
